512 devices in a mesh: dp: 8 (over x, core), label: 64 (over z, y).
Axes of the slice: x: 4, y: 8, z: 8, core: 2. Of those that a mesh axis runs over, the one named last changes fastest.
Arguments:
- embed: bfloat16 [8192, 768], P('dp'), may hold values from -6 to 6
- weight: bfloat16 [65536, 768], P('label'), may hold values from -0.21875 to 0.21875
- bias: bfloat16 [65536], P('label'), may hold values from -4 to 4
- beam: int32 [64, 134], P('dp'), may hold values from 0 to 511, as said below
- positives: int32 [8192, 8], P('dp'), may hold values from 0 to 65535, as said below
Outputs:
- row_grads: bfloat16 [8192, 768], P(('dp', 'label'))
- label_grads: bfloat16 [65536, 768], P(('label', 'dp'))
The draws below stay inside these ranges and needn't reach their ends.
Inputs may be any that keep to these rules, and one draw needn't show every extreme that they name: `beam`: the label device of cluster c is c // 8. A block's 134 clusters are distinct. For the 8 blocks of one data shard, one label device holds exactly 8 of every block's clusters, and every other label device holds exactly 2 clusters of every block. `positives`: each is a label of one of the beam clusters of the instance's own block; repeats may occur.
All inputs are finite; a program needn't handle non-finite values.
Results may differ from the reference program's by a relative error of at most 0.015.
Values may be sent and summed in bfloat16 or wider, within the bound.
A program may use at most 64 MiB of HBM per device.

```python
import jax
import jax.numpy as jnp
from jax import lax

D = 768
INST_BLOCK = 128
CLUSTER = 128
HOT = 8
SIB = 2
BEAM = 134
POS = 8
BLK_DEV = 8
CL_DEV = 8
NBLK = 64
NINST = 8192
CLUSTERS = 512
LABELS = 65536
N_DP = 8
N_LABEL = 64


def beam_table(key):
    busy_key, hot_key, sib_key, shuffle_key = jax.random.split(key, 4)
    busy_dev = jax.random.randint(busy_key, (N_DP,), 0, N_LABEL)
    busy_of = jnp.repeat(busy_dev, BLK_DEV)
    hot_pick = jax.vmap(lambda sub_key: jax.random.permutation(sub_key, CL_DEV))(jax.random.split(hot_key, NBLK))[:, :HOT]
    hot_ids = busy_of[:, None] * CL_DEV + hot_pick
    others = (busy_of[:, None] + jnp.arange(1, N_LABEL, dtype=jnp.int32)[None, :]) % N_LABEL
    sib_pick = jax.vmap(lambda sub_key: jax.random.permutation(sub_key, CL_DEV))(jax.random.split(sib_key, NBLK * (N_LABEL - 1)))[:, :SIB]
    sib_pick = sib_pick.reshape(NBLK, N_LABEL - 1, SIB)
    other_ids = (others[:, :, None] * CL_DEV + sib_pick).reshape(NBLK, (N_LABEL - 1) * SIB)
    beam_ids = jnp.concatenate([hot_ids, other_ids], axis=1).astype(jnp.int32)
    shuffle = jax.vmap(lambda sub_key: jax.random.permutation(sub_key, BEAM))(jax.random.split(shuffle_key, NBLK))
    return jnp.take_along_axis(beam_ids, shuffle, axis=1)


def draw_beam(key, part):
    return beam_table(key)


def draw_positives(key, part):
    beam_ids = beam_table(key)
    key = jax.random.fold_in(key, 5)
    slot_key, label_key = jax.random.split(key)
    slot_no = jax.random.randint(slot_key, (NINST, POS), 0, BEAM)
    within = jax.random.randint(label_key, (NINST, POS), 0, CLUSTER)
    block_of = jnp.arange(NINST, dtype=jnp.int32) // INST_BLOCK
    chosen = beam_ids[block_of[:, None], slot_no]
    return (chosen * CLUSTER + within).astype(jnp.int32)


def level_of(own_key, extent, shards, low, largest):
    loudness = 1.0
    for dim, shards_of in shards:
        draws = jax.random.uniform(jax.random.fold_in(jax.random.fold_in(own_key, 6), dim), (shards_of,), jnp.float32, low / len(shards), largest / len(shards))
        loudness = loudness * jnp.repeat(jnp.exp(draws), extent[dim] // shards_of).reshape((-1,) + (1,) * (len(extent) - 1 - dim))
    return loudness


def gaussian(rng, dims, width, most, cuts=(), held_as=jnp.bfloat16):
    values = width * jax.random.normal(rng, dims, jnp.float32)
    if cuts:
        values = values * level_of(rng, dims, cuts, -0.22, 0.18)
    return jnp.clip(values, -most, most).astype(held_as)


def setup_inputs(seed: int = 0) -> dict:
    key_of = jax.random.split(jax.random.key(seed), 6)
    return {
        "embed": gaussian(key_of[0], (NINST, D), 1.0, 6.0, ((0, 8),)),
        "weight": gaussian(key_of[1], (LABELS, D), D ** -0.5, 0.21875, ((0, 64),)),
        "bias": gaussian(key_of[2], (LABELS,), 1.0, 4.0, ((0, 64),)),
        "beam": draw_beam(jax.random.fold_in(key_of[5], 71), 0),
        "positives": draw_positives(jax.random.fold_in(key_of[5], 71), 0),
    }


grad_scale = 0.125


def block_terms(block_rows, positive_rows, beam_row, slabs, biases):
    chosen = slabs[beam_row]
    flattened = chosen.reshape(BEAM * CLUSTER, D)
    bias_row = biases[beam_row].reshape(BEAM * CLUSTER).astype(jnp.float32)
    scores = jnp.dot(block_rows, flattened.T, preferred_element_type=jnp.float32) + bias_row[None, :]
    labels = (beam_row[:, None] * CLUSTER + jnp.arange(CLUSTER, dtype=jnp.int32)[None, :]).reshape(BEAM * CLUSTER)
    target = jnp.any(positive_rows[:, :, None] == labels[None, None, :], axis=1).astype(jnp.float32)
    slopes = ((jax.nn.sigmoid(scores) - target) * grad_scale).astype(jnp.bfloat16)
    row_term = jnp.dot(slopes, flattened, preferred_element_type=jnp.float32)
    label_term = jnp.dot(slopes.T, block_rows, preferred_element_type=jnp.float32).reshape(BEAM, CLUSTER, D)
    return row_term, label_term


def reference(embed, weight, bias, beam, positives):
    slabs = weight.reshape(CLUSTERS, CLUSTER, D)
    biases = bias.reshape(CLUSTERS, CLUSTER)
    blocks = embed.reshape(NBLK, INST_BLOCK, D)
    wanted = positives.reshape(NBLK, INST_BLOCK, POS)
    row_parts = []
    label_total = jnp.zeros((CLUSTERS, CLUSTER, D), jnp.float32)
    for shard_no in range(N_DP):
        first_block = shard_no * BLK_DEV

        def visit_block(label_acc, local_block):
            block_id = first_block + local_block
            beam_row = beam[block_id]
            row_term, label_term = block_terms(blocks[block_id], wanted[block_id], beam_row, slabs, biases)
            label_acc = label_acc.at[beam_row].add(label_term)
            return label_acc, row_term

        label_acc, row_acc = lax.scan(visit_block, jnp.zeros((CLUSTERS, CLUSTER, D), jnp.float32), jnp.arange(BLK_DEV, dtype=jnp.int32))
        row_parts.append(row_acc)
        rounded = lax.optimization_barrier(label_acc.astype(jnp.bfloat16))
        label_total = label_total + rounded.astype(jnp.float32)
    row_grads = jnp.concatenate(row_parts, axis=0).reshape(NINST, D).astype(jnp.bfloat16)
    label_grads = label_total.reshape(LABELS, D).astype(jnp.bfloat16)
    return row_grads, label_grads
```

```python
import jax
import jax.numpy as jnp
from jax import lax
from jax.experimental import pallas as pl
from jax.experimental.pallas import tpu as pltpu
from jax.sharding import PartitionSpec as P

CLUSTER = 128
RING = 8
XRING = 4
HALF = 384
NT = (((1,), (1,)), ((), ()))
MESH = pl.DeviceIdType.MESH


def mark_targets(pos_ref, marks, base):
    for blk in range(8):
        local = pos_ref[:, blk * 128 : (blk + 1) * 128] - base
        inside = (local >= 0) & (local < 1024)
        low = local & 127
        bit = jnp.where(inside, jnp.left_shift(1, (local >> 7) & 7), 0)
        lanes = lax.broadcasted_iota(jnp.int32, (128, 128), 0)
        found = jnp.zeros((128, 128), jnp.int32)
        for p in range(8):
            found = found | jnp.where(lanes == low[p : p + 1, :], bit[p : p + 1, :], 0)
        marks[blk * 128 : (blk + 1) * 128, :] = found.T


def scale_pairs(beam_ref, scale, first):
    beam = beam_ref[...]
    for j in range(8):
        hit = jnp.max(jnp.where(beam == first + j, 0.0625, 0.0), axis=1, keepdims=True)
        scale[:, j * 128 : (j + 1) * 128] = jnp.broadcast_to(hit, (8, 128))


def make_slopes(embed_ref, weight_ref, bias_ref, marks, scale, slope, slope_t):
    half_bias = bias_ref[...].astype(jnp.float32) * 0.5
    for nb in range(4):
        scores = lax.dot_general(
            embed_ref[...], weight_ref[nb * 256 : (nb + 1) * 256, :], NT, preferred_element_type=jnp.float32
        )
        for h in range(2):
            j = 2 * nb + h
            cols = slice(j * 128, (j + 1) * 128)
            bent = jnp.tanh(scores[:, h * 128 : (h + 1) * 128] * 0.5 + half_bias[j : j + 1, :])
            sign = jnp.where((marks[...] & (1 << j)) != 0, -1.0, 1.0)
            value = (bent + sign).reshape(8, 128, 128) * scale[:, cols][:, None, :]
            value = value.reshape(1024, 128)
            slope[:, cols] = value.astype(jnp.bfloat16)
            slope_t[cols, :] = value.T.astype(jnp.bfloat16)


def kernel(
    embed_ref,
    weight_ref,
    bias_ref,
    beam_ref,
    pos_ref,
    row_ref,
    label_ref,
    marks,
    scale,
    slope,
    slope_t,
    rows,
    labels,
    a_out,
    a_in,
    b_out,
    b_in,
    a_piece,
    a_got,
    b_piece,
    b_got,
    c_out,
    c_in,
    x_out,
    x_in,
    ring_send,
    ring_recv,
    piece_send,
    piece_recv,
    c_send,
    c_recv,
    x_send,
    x_recv,
):
    dp = lax.axis_index("dp")
    label = lax.axis_index("label")
    z, y = label // RING, label % RING
    x, core = dp // 2, dp % 2

    def at_z(step):
        return (dp, ((z + step + RING) % RING) * RING + y)

    def at_y(step):
        return (dp, z * RING + (y + step + RING) % RING)

    def at_x(step):
        return (((x + step + XRING) % XRING) * 2 + core, label)

    sibling = (x * 2 + (1 - core), label)

    barrier = pltpu.get_barrier_semaphore()
    partners = [at_z(d) for d in range(1, 8)] + [at_y(d) for d in range(1, 8)] + [at_x(1), at_x(-1), sibling]
    for partner in partners:
        pl.semaphore_signal(barrier, inc=1, device_id=partner, device_id_type=MESH)

    scale_pairs(beam_ref, scale, label * 8)
    mark_targets(pos_ref, marks, label * 1024)
    make_slopes(embed_ref, weight_ref, bias_ref, marks, scale, slope, slope_t)
    for t in range(3):
        rows[:, :, :, t * 256 : (t + 1) * 256] = jnp.dot(
            slope[...], weight_ref[:, t * 256 : (t + 1) * 256], preferred_element_type=jnp.float32
        ).reshape(8, 8, 16, 256)

    pl.semaphore_wait(barrier, len(partners))

    started = []

    def send(src, dst, send_sem, recv_sem, device):
        copy = pltpu.make_async_remote_copy(
            src_ref=src, dst_ref=dst, send_sem=send_sem, recv_sem=recv_sem, device_id=device, device_id_type=MESH
        )
        copy.start()
        started.append(copy)
        return copy

    def part_a(c):
        return rows[c, :, :, 0:HALF]

    def part_b(c):
        return rows[:, c, :, HALF:]

    chains = []
    for kind in range(2):
        for side in range(2):
            chains.append((kind, side))

    flights = {}

    def ring_step(kind, side, d):
        out, came = (a_out, a_in) if kind == 0 else (b_out, b_in)
        here = z if kind == 0 else y
        step = 1 if side == 0 else -1
        c = (here + step * d + RING) % RING
        total = part_a(c) if kind == 0 else part_b(c)
        device = at_z(step) if kind == 0 else at_y(step)
        slot = 4 - d
        lo = 4 * side
        if d == 4:
            out[side, 0, lo : lo + 4] = total[lo : lo + 4].astype(jnp.bfloat16)
            src, dst = out.at[side, 0, lo : lo + 4], came.at[side, 0, lo : lo + 4]
        else:
            flights[kind, side, d + 1].wait_recv()
            if d == 3:
                out[side, 1] = total.astype(jnp.bfloat16)
                out[side, 1, lo : lo + 4] = (
                    total[lo : lo + 4] + came[side, 0, lo : lo + 4].astype(jnp.float32)
                ).astype(jnp.bfloat16)
            else:
                out[side, slot] = (total + came[side, slot - 1].astype(jnp.float32)).astype(jnp.bfloat16)
            src, dst = out.at[side, slot], came.at[side, slot]
        sem = (kind * 2 + side) * 4 + slot
        flights[kind, side, d] = send(src, dst, ring_send.at[sem], ring_recv.at[sem], device)

    for kind, side in chains:
        ring_step(kind, side, 4)

    other = 1 - core
    c_flights = []
    for k in range(4):
        j = 2 * k + other
        c_out[k] = jnp.dot(
            slope_t[pl.ds(pl.multiple_of(j * 128, 128), 128), :], embed_ref[...], preferred_element_type=jnp.float32
        ).astype(jnp.bfloat16)
        c_flights.append(send(c_out.at[k], c_in.at[k], c_send.at[k], c_recv.at[k], sibling))

    for kind, side in chains:
        ring_step(kind, side, 3)

    for k in range(4):
        j = 2 * k + core
        labels[k] = jnp.dot(
            slope_t[pl.ds(pl.multiple_of(j * 128, 128), 128), :], embed_ref[...], preferred_element_type=jnp.float32
        )
    for kind, side in chains:
        ring_step(kind, side, 2)

    for k in range(4):
        c_flights[k].wait_recv()
        labels[k] = labels[k] + c_in[k].astype(jnp.float32)

    x_flights = {}
    for side in range(2):
        c = (x + 2) % XRING
        lo = 64 * side
        x_out[side, 0, lo : lo + 64] = labels[c, lo : lo + 64].astype(jnp.bfloat16)
        x_flights[side, 2] = send(
            x_out.at[side, 0, lo : lo + 64],
            x_in.at[side, 0, lo : lo + 64],
            x_send.at[side * 2],
            x_recv.at[side * 2],
            at_x(1 - 2 * side),
        )
    for kind, side in chains:
        ring_step(kind, side, 1)
    for side in range(2):
        c = (x + 1 - 2 * side + XRING) % XRING
        lo = 64 * side
        rest = 64 - lo
        x_flights[side, 2].wait_recv()
        x_out[side, 1, lo : lo + 64] = (
            labels[c, lo : lo + 64] + x_in[side, 0, lo : lo + 64].astype(jnp.float32)
        ).astype(jnp.bfloat16)
        x_out[side, 1, rest : rest + 64] = labels[c, rest : rest + 64].astype(jnp.bfloat16)
        x_flights[side, 1] = send(
            x_out.at[side, 1],
            x_in.at[side, 1],
            x_send.at[side * 2 + 1],
            x_recv.at[side * 2 + 1],
            at_x(1 - 2 * side),
        )

    pieces = []
    for kind in range(2):
        came = a_in if kind == 0 else b_in
        piece, got = (a_piece, a_got) if kind == 0 else (b_piece, b_got)
        flights[kind, 0, 1].wait_recv()
        flights[kind, 1, 1].wait_recv()
        own = part_a(z) if kind == 0 else part_b(y)
        piece[...] = (own + came[0, 3].astype(jnp.float32) + came[1, 3].astype(jnp.float32)).astype(jnp.bfloat16)
        for d in range(1, RING):
            there = ((y if kind == 0 else z) + d) % RING
            sem = kind * 7 + d - 1
            pieces.append(
                send(
                    piece.at[there],
                    got.at[d - 1],
                    piece_send.at[sem],
                    piece_recv.at[sem],
                    at_y(d) if kind == 0 else at_z(d),
                )
            )

    for side in range(2):
        x_flights[side, 1].wait_recv()
    label_ref[...] = (labels[x] + x_in[0, 1].astype(jnp.float32) + x_in[1, 1].astype(jnp.float32)).astype(jnp.bfloat16)

    for copy in pieces:
        copy.wait_recv()
    for kind in range(2):
        piece, got = (a_piece, a_got) if kind == 0 else (b_piece, b_got)
        total = piece[y if kind == 0 else z].astype(jnp.float32)
        for d in range(7):
            total = total + got[d].astype(jnp.float32)
        row_ref[:, kind * HALF : (kind + 1) * HALF] = total.astype(jnp.bfloat16)
    for copy in started:
        copy.wait_send()


def on_device(embed, weight, bias, beam, positives):
    bf16, f32 = jnp.bfloat16, jnp.float32
    vmem = pl.BlockSpec(memory_space=pltpu.VMEM)
    return pl.pallas_call(
        kernel,
        out_shape=(jax.ShapeDtypeStruct((16, 768), bf16), jax.ShapeDtypeStruct((128, 768), bf16)),
        in_specs=[vmem] * 5,
        out_specs=(vmem, vmem),
        scratch_shapes=[
            pltpu.VMEM((1024, 128), jnp.int32),
            pltpu.VMEM((8, 1024), f32),
            pltpu.VMEM((1024, 1024), bf16),
            pltpu.VMEM((1024, 1024), bf16),
            pltpu.VMEM((8, 8, 16, 768), f32),
            pltpu.VMEM((4, 128, 768), f32),
            pltpu.VMEM((2, 4, 8, 16, HALF), bf16),
            pltpu.VMEM((2, 4, 8, 16, HALF), bf16),
            pltpu.VMEM((2, 4, 8, 16, HALF), bf16),
            pltpu.VMEM((2, 4, 8, 16, HALF), bf16),
            pltpu.VMEM((8, 16, HALF), bf16),
            pltpu.VMEM((7, 16, HALF), bf16),
            pltpu.VMEM((8, 16, HALF), bf16),
            pltpu.VMEM((7, 16, HALF), bf16),
            pltpu.VMEM((4, 128, 768), bf16),
            pltpu.VMEM((4, 128, 768), bf16),
            pltpu.VMEM((2, 2, 128, 768), bf16),
            pltpu.VMEM((2, 2, 128, 768), bf16),
            pltpu.SemaphoreType.DMA((16,)),
            pltpu.SemaphoreType.DMA((16,)),
            pltpu.SemaphoreType.DMA((14,)),
            pltpu.SemaphoreType.DMA((14,)),
            pltpu.SemaphoreType.DMA((4,)),
            pltpu.SemaphoreType.DMA((4,)),
            pltpu.SemaphoreType.DMA((4,)),
            pltpu.SemaphoreType.DMA((4,)),
        ],
        compiler_params=pltpu.CompilerParams(
            collective_id=0, has_side_effects=True, vmem_limit_bytes=56 * 1024 * 1024
        ),
        cost_estimate=pl.CostEstimate(flops=6 * 1024 * 1024 * 768, bytes_accessed=4 * 1024 * 1024, transcendentals=1024 * 1024),
    )(embed, weight, bias.reshape(8, 128), beam, positives.T)


def solution(mesh):
    in_specs = (P("dp", None), P("label", None), P("label"), P("dp", None), P("dp", None))
    out_specs = (P(("dp", "label"), None), P(("label", "dp"), None))
    return jax.shard_map(on_device, mesh=mesh, in_specs=in_specs, out_specs=out_specs, check_vma=False)
```

```python
import jax
import jax.numpy as jnp
from jax import lax
from jax.experimental import pallas as pl
from jax.experimental.pallas import tpu as pltpu
from jax.sharding import PartitionSpec as P

CLUSTER = 128
RING = 8
XRING = 4
HALF = 384
SUBS = 2
PER = RING // SUBS
NT = (((1,), (1,)), ((), ()))
MESH = pl.DeviceIdType.MESH


def mark_targets(pos_ref, marks, base):
    for blk in range(8):
        local = pos_ref[:, blk * 128 : (blk + 1) * 128] - base
        inside = (local >= 0) & (local < 1024)
        low = local & 127
        bit = jnp.where(inside, jnp.left_shift(1, (local >> 7) & 7), 0)
        lanes = lax.broadcasted_iota(jnp.int32, (128, 128), 0)
        found = jnp.zeros((128, 128), jnp.int32)
        for p in range(8):
            found = found | jnp.where(lanes == low[p : p + 1, :], bit[p : p + 1, :], 0)
        marks[blk * 128 : (blk + 1) * 128, :] = found.T


def scale_pairs(beam_ref, scale, first):
    beam = beam_ref[...]
    for j in range(8):
        hit = jnp.max(jnp.where(beam == first + j, 0.0625, 0.0), axis=1, keepdims=True)
        scale[:, j * 128 : (j + 1) * 128] = jnp.broadcast_to(hit, (8, 128))


def bend(scores, half_bias, marks, scale, j, groups):
    size = scores.shape[0] // groups
    bent = jnp.tanh(scores * 0.5 + half_bias[j : j + 1, :])
    sign = jnp.where((marks & (1 << j)) != 0, -1.0, 1.0)
    value = (bent + sign).reshape(groups, size, CLUSTER) * scale[:, None, :]
    return value.reshape(groups * size, CLUSTER)


def kernel(
    embed_hbm,
    weight_hbm,
    bias_ref,
    beam_ref,
    pos_ref,
    row_ref,
    label_ref,
    embed,
    weight,
    marks,
    scale,
    slope,
    slope_t,
    rows,
    labels,
    first_embed,
    first_marks,
    first_scale,
    first_slope,
    first_rows,
    ring_out,
    ring_in,
    piece,
    got,
    c_out,
    c_in,
    x_out,
    x_in,
    load_sem,
    ring_send,
    ring_recv,
    piece_send,
    piece_recv,
    c_send,
    c_recv,
    x_send,
    x_recv,
):
    f32, bf16 = jnp.float32, jnp.bfloat16
    loads = [pltpu.make_async_copy(embed_hbm, embed, load_sem.at[4])]
    loads += [
        pltpu.make_async_copy(weight_hbm.at[n * 256 : (n + 1) * 256], weight.at[n * 256 : (n + 1) * 256], load_sem.at[n])
        for n in range(4)
    ]
    for load in loads:
        load.start()

    dp = lax.axis_index("dp")
    label = lax.axis_index("label")
    z, y = label // RING, label % RING
    x, core = dp // 2, dp % 2

    def at_z(step):
        return (dp, ((z + step + RING) % RING) * RING + y)

    def at_y(step):
        return (dp, z * RING + (y + step + RING) % RING)

    def at_x(step):
        return (((x + step + XRING) % XRING) * 2 + core, label)

    sibling = (x * 2 + (1 - core), label)

    barrier = pltpu.get_barrier_semaphore()
    partners = [at_z(d) for d in range(1, 8)] + [at_y(d) for d in range(1, 8)] + [at_x(1), at_x(-1), sibling]
    for partner in partners:
        pl.semaphore_signal(barrier, inc=1, device_id=partner, device_id_type=MESH)

    scale_pairs(beam_ref, scale, label * 8)
    mark_targets(pos_ref, marks, label * 1024)
    half_bias = bias_ref[...].astype(f32) * 0.5

    def place(kind, chunk, r):
        return (chunk, (y + r) % RING) if kind == 0 else ((z + r) % RING, chunk)

    def chunk_at(kind, step):
        return ((z if kind == 0 else y) + step + RING) % RING

    loads[0].wait()
    for kind in range(2):
        for r in range(RING):
            b, q = place(kind, chunk_at(kind, 4), r)
            first_embed[kind * 8 + r] = embed[b, q]
            first_marks[kind * 8 + r] = marks[pl.ds(pl.multiple_of(b * 128 + q * 16, 16), 16), :]
            first_scale[kind * 8 + r : kind * 8 + r + 1, :] = scale[pl.ds(b, 1), :]
    for nb in range(4):
        loads[1 + nb].wait()
        scores = lax.dot_general(
            first_embed[...].reshape(256, 768), weight[nb * 256 : (nb + 1) * 256, :], NT, preferred_element_type=f32
        )
        for h in range(2):
            j = 2 * nb + h
            cols = slice(j * 128, (j + 1) * 128)
            first_slope[:, cols] = bend(
                scores[:, h * 128 : (h + 1) * 128],
                half_bias,
                first_marks[...].reshape(256, 128),
                first_scale[:, cols],
                j,
                16,
            ).astype(bf16)
    for kind in range(2):
        first_rows[kind] = jnp.dot(
            first_slope[kind * 128 : (kind + 1) * 128, :],
            weight[:, kind * HALF : (kind + 1) * HALF],
            preferred_element_type=f32,
        ).reshape(8, 16, HALF)

    started = []

    def send(src, dst, send_sem, recv_sem, device):
        copy = pltpu.make_async_remote_copy(
            src_ref=src, dst_ref=dst, send_sem=send_sem, recv_sem=recv_sem, device_id=device, device_id_type=MESH
        )
        copy.start()
        started.append(copy)
        return copy

    flights = {}

    def ring_step(kind, side, d, u):
        step = 1 if side == 0 else -1
        chunk = chunk_at(kind, step * d)
        slot = 4 - d
        key = (kind, side, d + 1, u)
        if key in flights:
            flights[key].wait_recv()
        for r in range(u * PER, (u + 1) * PER):
            if d == 4:
                total = first_rows[kind, r]
            else:
                b, q = place(kind, chunk, r)
                total = rows[b, q, :, kind * HALF : (kind + 1) * HALF]
            if key in flights:
                total = total + ring_in[kind, side, slot - 1, r].astype(f32)
            ring_out[kind, side, slot, r] = total.astype(bf16)
        part = (kind, side, slot, slice(u * PER, (u + 1) * PER))
        sem = ((kind * 2 + side) * 4 + slot) * SUBS + u
        flights[kind, side, d, u] = send(
            ring_out.at[part],
            ring_in.at[part],
            ring_send.at[sem],
            ring_recv.at[sem],
            at_z(step) if kind == 0 else at_y(step),
        )

    def is_long(side, u):
        return u // (SUBS // 2) == side

    def wave(d, long):
        for n in range(SUBS // 2):
            for side in range(2):
                for kind in range(2):
                    u = (side if long else 1 - side) * (SUBS // 2) + n
                    ring_step(kind, side, d, u)

    pl.semaphore_wait(barrier, len(partners))
    wave(4, True)

    for nb in range(4):
        scores = lax.dot_general(
            embed[...].reshape(1024, 768), weight[nb * 256 : (nb + 1) * 256, :], NT, preferred_element_type=f32
        )
        for h in range(2):
            j = 2 * nb + h
            cols = slice(j * 128, (j + 1) * 128)
            value = bend(scores[:, h * 128 : (h + 1) * 128], half_bias, marks[...], scale[:, cols], j, 8)
            slope[:, cols] = value.astype(bf16)
            slope_t[cols, :] = value.T.astype(bf16)
    for t in range(3):
        cols = slice(t * 256, (t + 1) * 256)
        rows[:, :, :, cols] = jnp.dot(slope[...], weight[:, cols], preferred_element_type=f32).reshape(8, 8, 16, 256)

    wave(3, False)
    wave(3, True)

    order = [(x + 2) % XRING, (x + 1) % XRING, (x + 3) % XRING, x]

    def label_part(j):
        return jnp.dot(
            slope_t[pl.ds(pl.multiple_of(j * 128, 128), 128), :], embed[...].reshape(1024, 768), preferred_element_type=f32
        )

    c_flights = []
    for n, k in enumerate(order):
        c_out[n] = label_part(2 * k + 1 - core).astype(bf16)
        c_flights.append(send(c_out.at[n], c_in.at[n], c_send.at[n], c_recv.at[n], sibling))
    for n, k in enumerate(order):
        labels[n] = label_part(2 * k + core)

    x_flights = {}

    def x_step(side, d, u):
        n = 0 if d == 2 else 1 + side
        part = slice(u * 64, (u + 1) * 64)
        total = labels[n, part]
        slot = (2 - d) * 2 + u
        if (side, 2, u) in x_flights:
            x_flights[side, 2, u].wait_recv()
            total = total + x_in[side, u].astype(f32)
        x_out[side, slot] = total.astype(bf16)
        x_flights[side, d, u] = send(
            x_out.at[side, slot],
            x_in.at[side, slot],
            x_send.at[side * 4 + slot],
            x_recv.at[side * 4 + slot],
            at_x(1 - 2 * side),
        )

    for n in range(4):
        c_flights[n].wait_recv()
        labels[n] = labels[n] + c_in[n].astype(f32)
        if n == 0:
            x_step(0, 2, 0)
            x_step(1, 2, 1)
        if n == 2:
            x_step(0, 1, 1)
            x_step(1, 1, 0)

    wave(2, False)
    wave(2, True)
    wave(1, False)
    x_step(0, 1, 0)
    x_step(1, 1, 1)
    wave(1, True)

    pieces = []
    for u in range(SUBS):
        for kind in range(2):
            flights[kind, 0, 1, u].wait_recv()
            flights[kind, 1, 1, u].wait_recv()
            for r in range(u * PER, (u + 1) * PER):
                b, q = place(kind, chunk_at(kind, 0), r)
                total = rows[b, q, :, kind * HALF : (kind + 1) * HALF]
                total = total + ring_in[kind, 0, 3, r].astype(f32) + ring_in[kind, 1, 3, r].astype(f32)
                if r == 0:
                    first_rows[kind, 0] = total
                    continue
                piece[kind, r] = total.astype(bf16)
                sem = kind * 8 + r
                pieces.append(
                    send(
                        piece.at[kind, r],
                        got.at[kind, r],
                        piece_send.at[sem],
                        piece_recv.at[sem],
                        at_y(r) if kind == 0 else at_z(r),
                    )
                )

    for u in range(2):
        part = slice(u * 64, (u + 1) * 64)
        x_flights[0, 1, u].wait_recv()
        x_flights[1, 1, u].wait_recv()
        label_ref[part] = (labels[3, part] + x_in[0, 2 + u].astype(f32) + x_in[1, 2 + u].astype(f32)).astype(bf16)

    for copy in pieces:
        copy.wait_recv()
    for kind in range(2):
        total = first_rows[kind, 0]
        for r in range(1, RING):
            total = total + got[kind, r].astype(f32)
        row_ref[:, kind * HALF : (kind + 1) * HALF] = total.astype(bf16)
    for copy in started:
        copy.wait_send()


def hand_over(row_in, label_in, row_ref, label_ref):
    row_ref[...] = row_in[...]
    label_ref[...] = label_in[...]


def on_device(embed, weight, bias, beam, positives):
    bf16, f32 = jnp.bfloat16, jnp.float32
    vmem = pl.BlockSpec(memory_space=pltpu.VMEM)
    hbm = pl.BlockSpec(memory_space=pltpu.HBM)
    dma = pltpu.SemaphoreType.DMA
    outs = (jax.ShapeDtypeStruct((16, 768), bf16), jax.ShapeDtypeStruct((128, 768), bf16))
    found = pl.pallas_call(
        kernel,
        out_shape=outs,
        in_specs=[hbm, hbm, vmem, vmem, vmem],
        out_specs=(vmem, vmem),
        scratch_shapes=[
            pltpu.VMEM((8, 8, 16, 768), bf16),
            pltpu.VMEM((1024, 768), bf16),
            pltpu.VMEM((1024, 128), jnp.int32),
            pltpu.VMEM((8, 1024), f32),
            pltpu.VMEM((1024, 1024), bf16),
            pltpu.VMEM((1024, 1024), bf16),
            pltpu.VMEM((8, 8, 16, 768), f32),
            pltpu.VMEM((4, 128, 768), f32),
            pltpu.VMEM((16, 16, 768), bf16),
            pltpu.VMEM((16, 16, 128), jnp.int32),
            pltpu.VMEM((16, 1024), f32),
            pltpu.VMEM((256, 1024), bf16),
            pltpu.VMEM((2, 8, 16, HALF), f32),
            pltpu.VMEM((2, 2, 4, 8, 16, HALF), bf16),
            pltpu.VMEM((2, 2, 4, 8, 16, HALF), bf16),
            pltpu.VMEM((2, 8, 16, HALF), bf16),
            pltpu.VMEM((2, 8, 16, HALF), bf16),
            pltpu.VMEM((4, 128, 768), bf16),
            pltpu.VMEM((4, 128, 768), bf16),
            pltpu.VMEM((2, 4, 64, 768), bf16),
            pltpu.VMEM((2, 4, 64, 768), bf16),
            dma((5,)),
            dma((16 * SUBS,)),
            dma((16 * SUBS,)),
            dma((16,)),
            dma((16,)),
            dma((4,)),
            dma((4,)),
            dma((8,)),
            dma((8,)),
        ],
        compiler_params=pltpu.CompilerParams(
            collective_id=0, has_side_effects=True, vmem_limit_bytes=56 * 1024 * 1024
        ),
        cost_estimate=pl.CostEstimate(
            flops=6 * 1024 * 1024 * 768, bytes_accessed=4 * 1024 * 1024, transcendentals=1024 * 1024
        ),
    )(embed.reshape(8, 8, 16, 768), weight, bias.reshape(8, 128), beam, positives.T)
    return pl.pallas_call(hand_over, out_shape=outs, in_specs=[vmem, vmem], out_specs=(vmem, vmem))(*found)


def solution(mesh):
    in_specs = (P("dp", None), P("label", None), P("label"), P("dp", None), P("dp", None))
    out_specs = (P(("dp", "label"), None), P(("label", "dp"), None))
    return jax.shard_map(on_device, mesh=mesh, in_specs=in_specs, out_specs=out_specs, check_vma=False)
```

```python
import jax
import jax.numpy as jnp
from jax import lax
from jax.experimental import pallas as pl
from jax.experimental.pallas import tpu as pltpu
from jax.sharding import PartitionSpec as P

CLUSTER = 128
RING = 8
XRING = 4
HALF = 384
SUBS = 2
PER = RING // SUBS
NEXT = {4: 2, 3: 2, 2: 0, 1: 0}
NT = (((1,), (1,)), ((), ()))
MESH = pl.DeviceIdType.MESH


def mark_targets(pos_ref, marks, base):
    for blk in range(8):
        local = pos_ref[:, blk * 128 : (blk + 1) * 128] - base
        inside = (local >= 0) & (local < 1024)
        low = local & 127
        bit = jnp.where(inside, jnp.left_shift(1, (local >> 7) & 7), 0)
        lanes = lax.broadcasted_iota(jnp.int32, (128, 128), 0)
        found = jnp.zeros((128, 128), jnp.int32)
        for p in range(8):
            found = found | jnp.where(lanes == low[p : p + 1, :], bit[p : p + 1, :], 0)
        marks[blk * 128 : (blk + 1) * 128, :] = found.T


def scale_pairs(beam_ref, scale, first):
    beam = beam_ref[...]
    for j in range(8):
        hit = jnp.max(jnp.where(beam == first + j, 0.0625, 0.0), axis=1, keepdims=True)
        scale[:, j * 128 : (j + 1) * 128] = jnp.broadcast_to(hit, (8, 128))


def bend(scores, half_bias, marks, scale, j, groups):
    size = scores.shape[0] // groups
    bent = jnp.tanh(scores * 0.5 + half_bias[j : j + 1, :])
    sign = jnp.where((marks & (1 << j)) != 0, -1.0, 1.0)
    value = (bent + sign).reshape(groups, size, CLUSTER) * scale[:, None, :]
    return value.reshape(groups * size, CLUSTER)


def kernel(
    embed_hbm,
    weight_hbm,
    bias_hbm,
    beam_hbm,
    pos_hbm,
    row_ref,
    label_ref,
    embed,
    weight,
    bias_ref,
    beam_ref,
    pos_ref,
    marks,
    scale,
    slope,
    slope_t,
    rows,
    labels,
    first_embed,
    first_marks,
    first_scale,
    first_slope,
    first_rows,
    ring_out,
    ring_in,
    piece,
    got,
    c_out,
    c_in,
    x_out,
    x_in,
    load_sem,
    ring_send,
    ring_recv,
    piece_send,
    piece_recv,
    c_send,
    c_recv,
    x_send,
    x_recv,
):
    f32, bf16 = jnp.float32, jnp.bfloat16
    small = [
        pltpu.make_async_copy(pos_hbm, pos_ref, load_sem.at[5]),
        pltpu.make_async_copy(beam_hbm, beam_ref, load_sem.at[6]),
        pltpu.make_async_copy(bias_hbm, bias_ref, load_sem.at[7]),
    ]
    loads = [pltpu.make_async_copy(embed_hbm, embed, load_sem.at[4])]
    loads += [
        pltpu.make_async_copy(weight_hbm.at[n * 256 : (n + 1) * 256], weight.at[n * 256 : (n + 1) * 256], load_sem.at[n])
        for n in range(4)
    ]
    for load in small + loads:
        load.start()

    dp = lax.axis_index("dp")
    label = lax.axis_index("label")
    z, y = label // RING, label % RING
    x, core = dp // 2, dp % 2

    def at_z(step):
        return (dp, ((z + step + RING) % RING) * RING + y)

    def at_y(step):
        return (dp, z * RING + (y + step + RING) % RING)

    def at_x(step):
        return (((x + step + XRING) % XRING) * 2 + core, label)

    sibling = (x * 2 + (1 - core), label)

    barrier = pltpu.get_barrier_semaphore()
    partners = [at_z(d) for d in range(1, 8)] + [at_y(d) for d in range(1, 8)] + [at_x(1), at_x(-1), sibling]
    for partner in partners:
        pl.semaphore_signal(barrier, inc=1, device_id=partner, device_id_type=MESH)

    for load in small:
        load.wait()
    scale_pairs(beam_ref, scale, label * 8)
    mark_targets(pos_ref, marks, label * 1024)
    half_bias = bias_ref[...].astype(f32) * 0.5

    def place(kind, chunk, r):
        return (chunk, (y + r) % RING) if kind == 0 else ((z + r) % RING, chunk)

    def chunk_at(kind, step):
        return ((z if kind == 0 else y) + step + RING) % RING

    loads[0].wait()
    for kind in range(2):
        for r in range(RING):
            b, q = place(kind, chunk_at(kind, 4), r)
            first_embed[kind * 8 + r] = embed[b, q]
            first_marks[kind * 8 + r] = marks[pl.ds(pl.multiple_of(b * 128 + q * 16, 16), 16), :]
            first_scale[kind * 8 + r : kind * 8 + r + 1, :] = scale[pl.ds(b, 1), :]
    for nb in range(4):
        loads[1 + nb].wait()
        scores = lax.dot_general(
            first_embed[...].reshape(256, 768), weight[nb * 256 : (nb + 1) * 256, :], NT, preferred_element_type=f32
        )
        for h in range(2):
            j = 2 * nb + h
            cols = slice(j * 128, (j + 1) * 128)
            first_slope[:, cols] = bend(
                scores[:, h * 128 : (h + 1) * 128],
                half_bias,
                first_marks[...].reshape(256, 128),
                first_scale[:, cols],
                j,
                16,
            ).astype(bf16)
    for kind in range(2):
        first_rows[kind] = jnp.dot(
            first_slope[kind * 128 : (kind + 1) * 128, :],
            weight[:, kind * HALF : (kind + 1) * HALF],
            preferred_element_type=f32,
        ).reshape(8, 16, HALF)

    started = []

    def send(src, dst, send_sem, recv_sem, device):
        copy = pltpu.make_async_remote_copy(
            src_ref=src, dst_ref=dst, send_sem=send_sem, recv_sem=recv_sem, device_id=device, device_id_type=MESH
        )
        copy.start()
        started.append(copy)
        return copy

    flights = {}

    def is_long(side, u):
        return u // (SUBS // 2) == side

    def ring_step(kind, side, d, u):
        step = 1 if side == 0 else -1
        chunk = chunk_at(kind, step * d)
        slot = 4 - d
        before = [e for e in (4, 3, 2) if NEXT[e] == d and (e < 4 or is_long(side, u))]
        for e in before:
            flights[kind, side, e, u].wait_recv()
        for r in range(u * PER, (u + 1) * PER):
            if d == 4:
                total = first_rows[kind, r]
            else:
                b, q = place(kind, chunk, r)
                total = rows[b, q, :, kind * HALF : (kind + 1) * HALF]
            for e in before:
                total = total + ring_in[kind, side, 4 - e, r].astype(f32)
            ring_out[kind, side, slot, r] = total.astype(bf16)
        part = (kind, side, slot, slice(u * PER, (u + 1) * PER))
        sem = ((kind * 2 + side) * 4 + slot) * SUBS + u
        hops = step * (d - NEXT[d])
        flights[kind, side, d, u] = send(
            ring_out.at[part],
            ring_in.at[part],
            ring_send.at[sem],
            ring_recv.at[sem],
            at_z(hops) if kind == 0 else at_y(hops),
        )

    def wave(d, long):
        for n in range(SUBS // 2):
            for side in range(2):
                for kind in range(2):
                    u = (side if long else 1 - side) * (SUBS // 2) + n
                    ring_step(kind, side, d, u)

    def add_rows(steps):
        for kind in range(2):
            chunks = [chunk_at(kind, step) for step in steps]
            left = [slope[c] if kind == 0 else slope[:, c] for c in chunks]
            left = jnp.concatenate([part.reshape(128, 1024) for part in left], axis=0)
            cols = slice(kind * HALF, (kind + 1) * HALF)
            found = jnp.dot(left, weight[:, cols], preferred_element_type=f32)
            for n, c in enumerate(chunks):
                part = found[n * 128 : (n + 1) * 128].reshape(8, 16, HALF)
                if kind == 0:
                    rows[c, :, :, cols] = part
                else:
                    rows[:, c, :, cols] = part

    pl.semaphore_wait(barrier, len(partners))
    wave(4, True)

    for nb in range(4):
        scores = lax.dot_general(
            embed[...].reshape(1024, 768), weight[nb * 256 : (nb + 1) * 256, :], NT, preferred_element_type=f32
        )
        for h in range(2):
            j = 2 * nb + h
            cols = slice(j * 128, (j + 1) * 128)
            value = bend(scores[:, h * 128 : (h + 1) * 128], half_bias, marks[...], scale[:, cols], j, 8)
            slope[:, :, :, cols] = value.astype(bf16).reshape(8, 8, 16, 128)
            slope_t[cols, :] = value.T.astype(bf16)
    add_rows((3, -3))
    wave(3, False)
    wave(3, True)
    add_rows((1, -1))
    wave(1, False)
    wave(1, True)

    order = [(x + 2) % XRING, (x + 1) % XRING, (x + 3) % XRING, x]

    def label_part(j):
        return jnp.dot(
            slope_t[pl.ds(pl.multiple_of(j * 128, 128), 128), :], embed[...].reshape(1024, 768), preferred_element_type=f32
        )

    c_flights = []
    for n, k in enumerate(order):
        c_out[n] = label_part(2 * k + 1 - core).astype(bf16)
        c_flights.append(send(c_out.at[n], c_in.at[n], c_send.at[n], c_recv.at[n], sibling))
    add_rows((2, -2))
    add_rows((0,))
    for n, k in enumerate(order):
        labels[n] = label_part(2 * k + core)
    wave(2, False)
    wave(2, True)

    x_flights = {}

    def x_step(side, d, u):
        n = 0 if d == 2 else 1 + side
        part = slice(u * 64, (u + 1) * 64)
        total = labels[n, part]
        slot = (2 - d) * 2 + u
        if (side, 2, u) in x_flights:
            x_flights[side, 2, u].wait_recv()
            total = total + x_in[side, u].astype(f32)
        x_out[side, slot] = total.astype(bf16)
        x_flights[side, d, u] = send(
            x_out.at[side, slot],
            x_in.at[side, slot],
            x_send.at[side * 4 + slot],
            x_recv.at[side * 4 + slot],
            at_x(1 - 2 * side),
        )

    for n in range(4):
        c_flights[n].wait_recv()
        labels[n] = labels[n] + c_in[n].astype(f32)
        if n == 0:
            x_step(0, 2, 0)
            x_step(1, 2, 1)
        if n == 2:
            x_step(0, 1, 1)
            x_step(1, 1, 0)

    x_step(0, 1, 0)
    x_step(1, 1, 1)

    pieces = []
    for u in range(SUBS):
        for kind in range(2):
            ends = [(side, e) for side in range(2) for e in (1, 2) if NEXT[e] == 0]
            for side, e in ends:
                flights[kind, side, e, u].wait_recv()
            for r in range(u * PER, (u + 1) * PER):
                b, q = place(kind, chunk_at(kind, 0), r)
                total = rows[b, q, :, kind * HALF : (kind + 1) * HALF]
                for side, e in ends:
                    total = total + ring_in[kind, side, 4 - e, r].astype(f32)
                if r == 0:
                    first_rows[kind, 0] = total
                    continue
                piece[kind, r] = total.astype(bf16)
                sem = kind * 8 + r
                pieces.append(
                    send(
                        piece.at[kind, r],
                        got.at[kind, r],
                        piece_send.at[sem],
                        piece_recv.at[sem],
                        at_y(r) if kind == 0 else at_z(r),
                    )
                )

    for u in range(2):
        part = slice(u * 64, (u + 1) * 64)
        x_flights[0, 1, u].wait_recv()
        x_flights[1, 1, u].wait_recv()
        label_ref[part] = (labels[3, part] + x_in[0, 2 + u].astype(f32) + x_in[1, 2 + u].astype(f32)).astype(bf16)

    for copy in pieces:
        copy.wait_recv()
    for kind in range(2):
        total = first_rows[kind, 0]
        for r in range(1, RING):
            total = total + got[kind, r].astype(f32)
        row_ref[:, kind * HALF : (kind + 1) * HALF] = total.astype(bf16)
    for copy in started:
        copy.wait_send()


def hand_over(row_in, label_in, row_ref, label_ref):
    row_ref[...] = row_in[...]
    label_ref[...] = label_in[...]


def on_device(embed, weight, bias, beam, positives):
    bf16, f32 = jnp.bfloat16, jnp.float32
    vmem = pl.BlockSpec(memory_space=pltpu.VMEM)
    hbm = pl.BlockSpec(memory_space=pltpu.HBM)
    dma = pltpu.SemaphoreType.DMA
    outs = (jax.ShapeDtypeStruct((16, 768), bf16), jax.ShapeDtypeStruct((128, 768), bf16))
    found = pl.pallas_call(
        kernel,
        out_shape=outs,
        in_specs=[hbm] * 5,
        out_specs=(vmem, vmem),
        scratch_shapes=[
            pltpu.VMEM((8, 8, 16, 768), bf16),
            pltpu.VMEM((1024, 768), bf16),
            pltpu.VMEM((8, 128), bf16),
            pltpu.VMEM((8, 134), jnp.int32),
            pltpu.VMEM((8, 1024), jnp.int32),
            pltpu.VMEM((1024, 128), jnp.int32),
            pltpu.VMEM((8, 1024), f32),
            pltpu.VMEM((8, 8, 16, 1024), bf16),
            pltpu.VMEM((1024, 1024), bf16),
            pltpu.VMEM((8, 8, 16, 768), f32),
            pltpu.VMEM((4, 128, 768), f32),
            pltpu.VMEM((16, 16, 768), bf16),
            pltpu.VMEM((16, 16, 128), jnp.int32),
            pltpu.VMEM((16, 1024), f32),
            pltpu.VMEM((256, 1024), bf16),
            pltpu.VMEM((2, 8, 16, HALF), f32),
            pltpu.VMEM((2, 2, 4, 8, 16, HALF), bf16),
            pltpu.VMEM((2, 2, 4, 8, 16, HALF), bf16),
            pltpu.VMEM((2, 8, 16, HALF), bf16),
            pltpu.VMEM((2, 8, 16, HALF), bf16),
            pltpu.VMEM((4, 128, 768), bf16),
            pltpu.VMEM((4, 128, 768), bf16),
            pltpu.VMEM((2, 4, 64, 768), bf16),
            pltpu.VMEM((2, 4, 64, 768), bf16),
            dma((8,)),
            dma((16 * SUBS,)),
            dma((16 * SUBS,)),
            dma((16,)),
            dma((16,)),
            dma((4,)),
            dma((4,)),
            dma((8,)),
            dma((8,)),
        ],
        compiler_params=pltpu.CompilerParams(
            collective_id=0, has_side_effects=True, vmem_limit_bytes=56 * 1024 * 1024
        ),
        cost_estimate=pl.CostEstimate(
            flops=6 * 1024 * 1024 * 768, bytes_accessed=4 * 1024 * 1024, transcendentals=1024 * 1024
        ),
    )(embed.reshape(8, 8, 16, 768), weight, bias.reshape(8, 128), beam, positives.T)
    return pl.pallas_call(hand_over, out_shape=outs, in_specs=[vmem, vmem], out_specs=(vmem, vmem))(*found)


def solution(mesh):
    in_specs = (P("dp", None), P("label", None), P("label"), P("dp", None), P("dp", None))
    out_specs = (P(("dp", "label"), None), P(("label", "dp"), None))
    return jax.shard_map(on_device, mesh=mesh, in_specs=in_specs, out_specs=out_specs, check_vma=False)
```

```python
import jax
import jax.numpy as jnp
from jax import lax
from jax.experimental import pallas as pl
from jax.experimental.pallas import tpu as pltpu
from jax.sharding import PartitionSpec as P

CLUSTER = 128
RING = 8
XRING = 4
HALF = 384
SUBS = 2
PER = RING // SUBS
NEXT = {4: 2, 3: 2, 2: 0, 1: 0}
ROLL = (4, 3, 5, 2, 6, 1, 7, 0)
NT = (((1,), (1,)), ((), ()))
MESH = pl.DeviceIdType.MESH


def mark_targets(pos_ref, marks, base):
    for blk in range(8):
        local = pos_ref[:, blk * 128 : (blk + 1) * 128] - base
        inside = (local >= 0) & (local < 1024)
        low = local & 127
        bit = jnp.where(inside, jnp.left_shift(1, (local >> 7) & 7), 0)
        lanes = lax.broadcasted_iota(jnp.int32, (128, 128), 0)
        found = jnp.zeros((128, 128), jnp.int32)
        for p in range(8):
            found = found | jnp.where(lanes == low[p : p + 1, :], bit[p : p + 1, :], 0)
        marks[blk * 128 : (blk + 1) * 128, :] = found.T


def scale_pairs(beam_ref, scale, first):
    beam = beam_ref[...]
    for j in range(8):
        hit = jnp.max(jnp.where(beam == first + j, 0.0625, 0.0), axis=1, keepdims=True)
        scale[:, j * 128 : (j + 1) * 128] = jnp.broadcast_to(hit, (8, 128))


def bend(scores, half_bias, marks, scale, j, groups):
    size = scores.shape[0] // groups
    bent = jnp.tanh(scores * 0.5 + half_bias[j : j + 1, :])
    sign = jnp.where((marks & (1 << j)) != 0, -1.0, 1.0)
    value = (bent + sign).reshape(groups, size, CLUSTER) * scale[:, None, :]
    return value.reshape(groups * size, CLUSTER)


def kernel(
    embed_hbm,
    weight_hbm,
    bias_hbm,
    beam_hbm,
    pos_hbm,
    row_ref,
    label_ref,
    embed,
    weight,
    bias_ref,
    beam_ref,
    pos_ref,
    marks,
    scale,
    slope,
    slope_t,
    rows,
    labels,
    first_embed,
    first_marks,
    first_scale,
    first_slope,
    first_rows,
    ring_out,
    ring_in,
    piece,
    got,
    c_out,
    c_in,
    x_out,
    x_in,
    load_sem,
    ring_send,
    ring_recv,
    piece_send,
    piece_recv,
    c_send,
    c_recv,
    x_send,
    x_recv,
):
    f32, bf16 = jnp.float32, jnp.bfloat16
    small = [
        pltpu.make_async_copy(pos_hbm, pos_ref, load_sem.at[5]),
        pltpu.make_async_copy(beam_hbm, beam_ref, load_sem.at[6]),
        pltpu.make_async_copy(bias_hbm, bias_ref, load_sem.at[7]),
    ]
    label = lax.axis_index("label")
    z, y = label // RING, label % RING
    loads = [
        pltpu.make_async_copy(embed_hbm.at[(z + 4) % RING], first_embed.at[0:8], load_sem.at[8]),
        pltpu.make_async_copy(embed_hbm.at[:, (y + 4) % RING], first_embed.at[8:16], load_sem.at[9]),
    ]
    loads += [
        pltpu.make_async_copy(weight_hbm.at[n * 256 : (n + 1) * 256], weight.at[n * 256 : (n + 1) * 256], load_sem.at[n])
        for n in range(4)
    ]
    whole = pltpu.make_async_copy(embed_hbm, embed, load_sem.at[4])
    for load in small + loads + [whole]:
        load.start()

    dp = lax.axis_index("dp")
    x, core = dp // 2, dp % 2

    def at_z(step):
        return (dp, ((z + step + RING) % RING) * RING + y)

    def at_y(step):
        return (dp, z * RING + (y + step + RING) % RING)

    def at_x(step):
        return (((x + step + XRING) % XRING) * 2 + core, label)

    sibling = (x * 2 + (1 - core), label)

    barrier = pltpu.get_barrier_semaphore()
    partners = [at_z(d) for d in range(1, 8)] + [at_y(d) for d in range(1, 8)] + [at_x(1), at_x(-1), sibling]
    for partner in partners:
        pl.semaphore_signal(barrier, inc=1, device_id=partner, device_id_type=MESH)

    for load in small:
        load.wait()
    scale_pairs(beam_ref, scale, label * 8)
    mark_targets(pos_ref, marks, label * 1024)
    half_bias = bias_ref[...].astype(f32) * 0.5

    def place(kind, chunk, r):
        return (chunk, (y + r) % RING) if kind == 0 else ((z + r) % RING, chunk)

    def chunk_at(kind, step):
        return ((z if kind == 0 else y) + step + RING) % RING

    for n in range(RING):
        for kind, b, q in ((0, (z + 4) % RING, n), (1, n, (y + 4) % RING)):
            first_marks[kind * 8 + n] = marks[pl.ds(pl.multiple_of(b * 128 + q * 16, 16), 16), :]
            first_scale[kind * 8 + n : kind * 8 + n + 1, :] = scale[pl.ds(b, 1), :]
    loads[0].wait()
    loads[1].wait()
    for nb in range(4):
        loads[2 + nb].wait()
        scores = lax.dot_general(
            first_embed[...].reshape(256, 768), weight[nb * 256 : (nb + 1) * 256, :], NT, preferred_element_type=f32
        )
        for h in range(2):
            j = 2 * nb + h
            cols = slice(j * 128, (j + 1) * 128)
            first_slope[:, cols] = bend(
                scores[:, h * 128 : (h + 1) * 128],
                half_bias,
                first_marks[...].reshape(256, 128),
                first_scale[:, cols],
                j,
                16,
            ).astype(bf16)
    for kind in range(2):
        first_rows[kind] = jnp.dot(
            first_slope[kind * 128 : (kind + 1) * 128, :],
            weight[:, kind * HALF : (kind + 1) * HALF],
            preferred_element_type=f32,
        ).reshape(8, 16, HALF)

    started = []

    def send(src, dst, send_sem, recv_sem, device):
        copy = pltpu.make_async_remote_copy(
            src_ref=src, dst_ref=dst, send_sem=send_sem, recv_sem=recv_sem, device_id=device, device_id_type=MESH
        )
        copy.start()
        started.append(copy)
        return copy

    flights = {}

    def is_long(side, u):
        return u // (SUBS // 2) == side

    def ring_step(kind, side, d, u):
        step = 1 if side == 0 else -1
        chunk = chunk_at(kind, step * d)
        slot = 4 - d
        before = [e for e in (4, 3, 2) if NEXT[e] == d and (e < 4 or is_long(side, u))]
        for e in before:
            flights[kind, side, e, u].wait_recv()
        for r in range(u * PER, (u + 1) * PER):
            b, q = place(kind, chunk, ROLL[r])
            if d == 4:
                total = first_rows[kind, q if kind == 0 else b]
            else:
                total = rows[b, q, :, kind * HALF : (kind + 1) * HALF]
            for e in before:
                total = total + ring_in[kind, side, 4 - e, r].astype(f32)
            ring_out[kind, side, slot, r] = total.astype(bf16)
        part = (kind, side, slot, slice(u * PER, (u + 1) * PER))
        sem = ((kind * 2 + side) * 4 + slot) * SUBS + u
        hops = step * (d - NEXT[d])
        flights[kind, side, d, u] = send(
            ring_out.at[part],
            ring_in.at[part],
            ring_send.at[sem],
            ring_recv.at[sem],
            at_z(hops) if kind == 0 else at_y(hops),
        )

    def wave(d, u):
        for side in range(2):
            for kind in range(2):
                if d < 4 or is_long(side, u):
                    ring_step(kind, side, d, u)

    def add_rows(steps):
        for kind in range(2):
            chunks = [chunk_at(kind, step) for step in steps]
            left = [slope[c] if kind == 0 else slope[:, c] for c in chunks]
            left = jnp.concatenate([part.reshape(128, 1024) for part in left], axis=0)
            cols = slice(kind * HALF, (kind + 1) * HALF)
            found = jnp.dot(left, weight[:, cols], preferred_element_type=f32)
            for n, c in enumerate(chunks):
                part = found[n * 128 : (n + 1) * 128].reshape(8, 16, HALF)
                if kind == 0:
                    rows[c, :, :, cols] = part
                else:
                    rows[:, c, :, cols] = part

    pl.semaphore_wait(barrier, len(partners))
    wave(4, 0)
    wave(4, 1)

    whole.wait()
    for nb in range(4):
        scores = lax.dot_general(
            embed[...].reshape(1024, 768), weight[nb * 256 : (nb + 1) * 256, :], NT, preferred_element_type=f32
        )
        for h in range(2):
            j = 2 * nb + h
            cols = slice(j * 128, (j + 1) * 128)
            value = bend(scores[:, h * 128 : (h + 1) * 128], half_bias, marks[...], scale[:, cols], j, 8)
            slope[:, :, :, cols] = value.astype(bf16).reshape(8, 8, 16, 128)
            slope_t[cols, :] = value.T.astype(bf16)
    add_rows((3, -3))
    wave(3, 0)
    wave(3, 1)
    add_rows((1, -1))
    wave(1, 0)
    wave(1, 1)

    order = [(x + 2) % XRING, (x + 1) % XRING, (x + 3) % XRING, x]

    def label_part(j):
        return jnp.dot(
            slope_t[pl.ds(pl.multiple_of(j * 128, 128), 128), :], embed[...].reshape(1024, 768), preferred_element_type=f32
        )

    c_flights = []
    for n, k in enumerate(order):
        c_out[n] = label_part(2 * k + 1 - core).astype(bf16)
        c_flights.append(send(c_out.at[n], c_in.at[n], c_send.at[n], c_recv.at[n], sibling))
    add_rows((2, -2))
    add_rows((0,))
    for n, k in enumerate(order):
        labels[n] = label_part(2 * k + core)
    wave(2, 0)
    wave(2, 1)

    x_flights = {}

    def x_step(side, d, u):
        n = 0 if d == 2 else 1 + side
        part = slice(u * 64, (u + 1) * 64)
        total = labels[n, part]
        slot = (2 - d) * 2 + u
        if (side, 2, u) in x_flights:
            x_flights[side, 2, u].wait_recv()
            total = total + x_in[side, u].astype(f32)
        x_out[side, slot] = total.astype(bf16)
        x_flights[side, d, u] = send(
            x_out.at[side, slot],
            x_in.at[side, slot],
            x_send.at[side * 4 + slot],
            x_recv.at[side * 4 + slot],
            at_x(1 - 2 * side),
        )

    for n in range(4):
        c_flights[n].wait_recv()
        labels[n] = labels[n] + c_in[n].astype(f32)
        if n == 0:
            x_step(0, 2, 0)
            x_step(1, 2, 1)
        if n == 2:
            x_step(0, 1, 1)
            x_step(1, 1, 0)

    pieces = []
    for u in range(SUBS):
        if u == SUBS - 1:
            x_step(0, 1, 0)
            x_step(1, 1, 1)
        for kind in range(2):
            ends = [(side, e) for side in range(2) for e in (1, 2) if NEXT[e] == 0]
            for side, e in ends:
                flights[kind, side, e, u].wait_recv()
            for s in range(u * PER, (u + 1) * PER):
                r = ROLL[s]
                b, q = place(kind, chunk_at(kind, 0), r)
                total = rows[b, q, :, kind * HALF : (kind + 1) * HALF]
                for side, e in ends:
                    total = total + ring_in[kind, side, 4 - e, s].astype(f32)
                if r == 0:
                    first_rows[kind, 0] = total
                    continue
                piece[kind, r] = total.astype(bf16)
                sem = kind * 8 + r
                pieces.append(
                    send(
                        piece.at[kind, r],
                        got.at[kind, r],
                        piece_send.at[sem],
                        piece_recv.at[sem],
                        at_y(r) if kind == 0 else at_z(r),
                    )
                )

    for u in range(2):
        part = slice(u * 64, (u + 1) * 64)
        x_flights[0, 1, u].wait_recv()
        x_flights[1, 1, u].wait_recv()
        label_ref[part] = (labels[3, part] + x_in[0, 2 + u].astype(f32) + x_in[1, 2 + u].astype(f32)).astype(bf16)

    for copy in pieces:
        copy.wait_recv()
    for kind in range(2):
        total = first_rows[kind, 0]
        for r in range(1, RING):
            total = total + got[kind, r].astype(f32)
        row_ref[:, kind * HALF : (kind + 1) * HALF] = total.astype(bf16)
    for copy in started:
        copy.wait_send()


def hand_over(row_in, label_in, row_ref, label_ref):
    row_ref[...] = row_in[...]
    label_ref[...] = label_in[...]


def on_device(embed, weight, bias, beam, positives):
    bf16, f32 = jnp.bfloat16, jnp.float32
    vmem = pl.BlockSpec(memory_space=pltpu.VMEM)
    hbm = pl.BlockSpec(memory_space=pltpu.HBM)
    dma = pltpu.SemaphoreType.DMA
    outs = (jax.ShapeDtypeStruct((16, 768), bf16), jax.ShapeDtypeStruct((128, 768), bf16))
    found = pl.pallas_call(
        kernel,
        out_shape=outs,
        in_specs=[hbm] * 5,
        out_specs=(vmem, vmem),
        scratch_shapes=[
            pltpu.VMEM((8, 8, 16, 768), bf16),
            pltpu.VMEM((1024, 768), bf16),
            pltpu.VMEM((8, 128), bf16),
            pltpu.VMEM((8, 134), jnp.int32),
            pltpu.VMEM((8, 1024), jnp.int32),
            pltpu.VMEM((1024, 128), jnp.int32),
            pltpu.VMEM((8, 1024), f32),
            pltpu.VMEM((8, 8, 16, 1024), bf16),
            pltpu.VMEM((1024, 1024), bf16),
            pltpu.VMEM((8, 8, 16, 768), f32),
            pltpu.VMEM((4, 128, 768), f32),
            pltpu.VMEM((16, 16, 768), bf16),
            pltpu.VMEM((16, 16, 128), jnp.int32),
            pltpu.VMEM((16, 1024), f32),
            pltpu.VMEM((256, 1024), bf16),
            pltpu.VMEM((2, 8, 16, HALF), f32),
            pltpu.VMEM((2, 2, 4, 8, 16, HALF), bf16),
            pltpu.VMEM((2, 2, 4, 8, 16, HALF), bf16),
            pltpu.VMEM((2, 8, 16, HALF), bf16),
            pltpu.VMEM((2, 8, 16, HALF), bf16),
            pltpu.VMEM((4, 128, 768), bf16),
            pltpu.VMEM((4, 128, 768), bf16),
            pltpu.VMEM((2, 4, 64, 768), bf16),
            pltpu.VMEM((2, 4, 64, 768), bf16),
            dma((10,)),
            dma((16 * SUBS,)),
            dma((16 * SUBS,)),
            dma((16,)),
            dma((16,)),
            dma((4,)),
            dma((4,)),
            dma((8,)),
            dma((8,)),
        ],
        compiler_params=pltpu.CompilerParams(
            collective_id=0, has_side_effects=True, vmem_limit_bytes=56 * 1024 * 1024
        ),
        cost_estimate=pl.CostEstimate(
            flops=6 * 1024 * 1024 * 768, bytes_accessed=4 * 1024 * 1024, transcendentals=1024 * 1024
        ),
    )(embed.reshape(8, 8, 16, 768), weight, bias.reshape(8, 128), beam, positives.T)
    return pl.pallas_call(hand_over, out_shape=outs, in_specs=[vmem, vmem], out_specs=(vmem, vmem))(*found)


def solution(mesh):
    in_specs = (P("dp", None), P("label", None), P("label"), P("dp", None), P("dp", None))
    out_specs = (P(("dp", "label"), None), P(("label", "dp"), None))
    return jax.shard_map(on_device, mesh=mesh, in_specs=in_specs, out_specs=out_specs, check_vma=False)
```

```python
import jax
import jax.numpy as jnp
from jax import lax
from jax.experimental import pallas as pl
from jax.experimental.pallas import tpu as pltpu
from jax.sharding import PartitionSpec as P

CLUSTER = 128
RING = 8
XRING = 4
HALF = 384
SUBS = 2
PER = RING // SUBS
NEXT = {4: 2, 3: 2, 2: 0, 1: 0}
ROLL = (4, 3, 5, 2, 6, 1, 7, 0)
NT = (((1,), (1,)), ((), ()))
MESH = pl.DeviceIdType.MESH


def mark_targets(pos_ref, marks, base):
    for blk in range(8):
        local = pos_ref[:, blk * 128 : (blk + 1) * 128] - base
        inside = (local >= 0) & (local < 1024)
        low = local & 127
        bit = jnp.where(inside, jnp.left_shift(1, (local >> 7) & 7), 0)
        lanes = lax.broadcasted_iota(jnp.int32, (128, 128), 0)
        found = jnp.zeros((128, 128), jnp.int32)
        for p in range(8):
            found = found | jnp.where(lanes == low[p : p + 1, :], bit[p : p + 1, :], 0)
        marks[blk * 128 : (blk + 1) * 128, :] = found.T


def scale_pairs(beam_ref, scale, first):
    beam = beam_ref[...]
    for j in range(8):
        hit = jnp.max(jnp.where(beam == first + j, 0.0625, 0.0), axis=1, keepdims=True)
        scale[:, j * 128 : (j + 1) * 128] = jnp.broadcast_to(hit, (8, 128))


def bend(scores, half_bias, marks, scale, j, groups):
    size = scores.shape[0] // groups
    bent = jnp.tanh(scores * 0.5 + half_bias[j : j + 1, :])
    sign = jnp.where((marks & (1 << j)) != 0, -1.0, 1.0)
    value = (bent + sign).reshape(groups, size, CLUSTER) * scale[:, None, :]
    return value.reshape(groups * size, CLUSTER)


def kernel(
    embed_hbm,
    weight_hbm,
    bias_hbm,
    beam_hbm,
    pos_hbm,
    row_ref,
    label_ref,
    embed,
    weight,
    bias_ref,
    beam_ref,
    pos_ref,
    marks,
    scale,
    slope,
    slope_t,
    rows,
    labels,
    first_embed,
    first_marks,
    first_scale,
    first_slope,
    first_rows,
    ring_out,
    ring_in,
    piece,
    got,
    c_out,
    c_in,
    x_out,
    x_in,
    load_sem,
    ring_send,
    ring_recv,
    piece_send,
    piece_recv,
    c_send,
    c_recv,
    x_send,
    x_recv,
):
    f32, bf16 = jnp.float32, jnp.bfloat16
    small = [
        pltpu.make_async_copy(pos_hbm, pos_ref, load_sem.at[5]),
        pltpu.make_async_copy(beam_hbm, beam_ref, load_sem.at[6]),
        pltpu.make_async_copy(bias_hbm, bias_ref, load_sem.at[7]),
    ]
    label = lax.axis_index("label")
    z, y = label // RING, label % RING
    loads = [
        pltpu.make_async_copy(embed_hbm.at[(z + 4) % RING], first_embed.at[0:8], load_sem.at[8]),
        pltpu.make_async_copy(embed_hbm.at[:, (y + 4) % RING], first_embed.at[8:16], load_sem.at[9]),
    ]
    loads += [
        pltpu.make_async_copy(weight_hbm.at[n * 256 : (n + 1) * 256], weight.at[n * 256 : (n + 1) * 256], load_sem.at[n])
        for n in range(4)
    ]
    whole = pltpu.make_async_copy(embed_hbm, embed, load_sem.at[4])
    for load in small + loads + [whole]:
        load.start()

    dp = lax.axis_index("dp")
    x, core = dp // 2, dp % 2

    def at_z(step):
        return (dp, ((z + step + RING) % RING) * RING + y)

    def at_y(step):
        return (dp, z * RING + (y + step + RING) % RING)

    def at_x(step):
        return (((x + step + XRING) % XRING) * 2 + core, label)

    sibling = (x * 2 + (1 - core), label)

    barrier = pltpu.get_barrier_semaphore()
    partners = [at_z(d) for d in range(1, 8)] + [at_y(d) for d in range(1, 8)] + [at_x(1), at_x(-1), sibling]
    for partner in partners:
        pl.semaphore_signal(barrier, inc=1, device_id=partner, device_id_type=MESH)

    for load in small:
        load.wait()
    scale_pairs(beam_ref, scale, label * 8)
    mark_targets(pos_ref, marks, label * 1024)
    half_bias = bias_ref[...].astype(f32) * 0.5

    def place(kind, chunk, r):
        return (chunk, (y + r) % RING) if kind == 0 else ((z + r) % RING, chunk)

    def chunk_at(kind, step):
        return ((z if kind == 0 else y) + step + RING) % RING

    for n in range(RING):
        for kind, b, q in ((0, (z + 4) % RING, n), (1, n, (y + 4) % RING)):
            first_marks[kind * 8 + n] = marks[pl.ds(pl.multiple_of(b * 128 + q * 16, 16), 16), :]
            first_scale[kind * 8 + n : kind * 8 + n + 1, :] = scale[pl.ds(b, 1), :]
    loads[0].wait()
    loads[1].wait()
    for nb in range(4):
        loads[2 + nb].wait()
        scores = lax.dot_general(
            first_embed[...].reshape(256, 768), weight[nb * 256 : (nb + 1) * 256, :], NT, preferred_element_type=f32
        )
        for h in range(2):
            j = 2 * nb + h
            cols = slice(j * 128, (j + 1) * 128)
            first_slope[:, cols] = bend(
                scores[:, h * 128 : (h + 1) * 128],
                half_bias,
                first_marks[...].reshape(256, 128),
                first_scale[:, cols],
                j,
                16,
            ).astype(bf16)
    for kind in range(2):
        first_rows[kind] = jnp.dot(
            first_slope[kind * 128 : (kind + 1) * 128, :],
            weight[:, kind * HALF : (kind + 1) * HALF],
            preferred_element_type=f32,
        ).reshape(8, 16, HALF)

    started = []

    def send(src, dst, send_sem, recv_sem, device):
        copy = pltpu.make_async_remote_copy(
            src_ref=src, dst_ref=dst, send_sem=send_sem, recv_sem=recv_sem, device_id=device, device_id_type=MESH
        )
        copy.start()
        started.append(copy)
        return copy

    flights = {}

    def is_long(side, u):
        return u // (SUBS // 2) == side

    def ring_step(kind, side, d, u):
        step = 1 if side == 0 else -1
        chunk = chunk_at(kind, step * d)
        slot = 4 - d
        before = [e for e in (4, 3, 2) if NEXT[e] == d and (e < 4 or is_long(side, u))]
        for e in before:
            flights[kind, side, e, u].wait_recv()
        for r in range(u * PER, (u + 1) * PER):
            b, q = place(kind, chunk, ROLL[r])
            if d == 4:
                total = first_rows[kind, q if kind == 0 else b]
            else:
                total = rows[b, q, :, kind * HALF : (kind + 1) * HALF]
            for e in before:
                total = total + ring_in[kind, side, 4 - e, r].astype(f32)
            ring_out[kind, side, slot, r] = total.astype(bf16)
        part = (kind, side, slot, slice(u * PER, (u + 1) * PER))
        sem = ((kind * 2 + side) * 4 + slot) * SUBS + u
        hops = step * (d - NEXT[d])
        flights[kind, side, d, u] = send(
            ring_out.at[part],
            ring_in.at[part],
            ring_send.at[sem],
            ring_recv.at[sem],
            at_z(hops) if kind == 0 else at_y(hops),
        )

    def wave(d, u):
        for side in range(2):
            for kind in range(2):
                if d < 4 or is_long(side, u):
                    ring_step(kind, side, d, u)

    def add_rows(steps):
        for kind in range(2):
            chunks = [chunk_at(kind, step) for step in steps]
            left = [slope[c] if kind == 0 else slope[:, c] for c in chunks]
            left = jnp.concatenate([part.reshape(128, 1024) for part in left], axis=0)
            cols = slice(kind * HALF, (kind + 1) * HALF)
            found = jnp.dot(left, weight[:, cols], preferred_element_type=f32)
            for n, c in enumerate(chunks):
                part = found[n * 128 : (n + 1) * 128].reshape(8, 16, HALF)
                if kind == 0:
                    rows[c, :, :, cols] = part
                else:
                    rows[:, c, :, cols] = part

    pl.semaphore_wait(barrier, len(partners))
    wave(4, 0)
    wave(4, 1)

    whole.wait()
    for nb in range(4):
        scores = lax.dot_general(
            embed[...].reshape(1024, 768), weight[nb * 256 : (nb + 1) * 256, :], NT, preferred_element_type=f32
        )
        for h in range(2):
            j = 2 * nb + h
            cols = slice(j * 128, (j + 1) * 128)
            value = bend(scores[:, h * 128 : (h + 1) * 128], half_bias, marks[...], scale[:, cols], j, 8)
            slope[:, :, :, cols] = value.astype(bf16).reshape(8, 8, 16, 128)
            slope_t[cols, :] = value.T.astype(bf16)
    add_rows((3, -3))
    wave(3, 0)
    wave(3, 1)
    add_rows((1, -1))
    wave(1, 0)
    wave(1, 1)

    order = [(x + 2) % XRING, (x + 1) % XRING, (x + 3) % XRING, x]

    def label_part(j):
        return jnp.dot(
            slope_t[pl.ds(pl.multiple_of(j * 128, 128), 128), :], embed[...].reshape(1024, 768), preferred_element_type=f32
        )

    c_flights = []
    for n, k in enumerate(order):
        c_out[n] = label_part(2 * k + 1 - core).astype(bf16)
        c_flights.append(send(c_out.at[n], c_in.at[n], c_send.at[n], c_recv.at[n], sibling))
    add_rows((2, -2))
    add_rows((0,))
    for n, k in enumerate(order):
        labels[n] = label_part(2 * k + core)
    wave(2, 0)
    wave(2, 1)

    x_flights = {}

    def x_step(side, d, u):
        n = 0 if d == 2 else 1 + side
        part = slice(u * 64, (u + 1) * 64)
        total = labels[n, part]
        slot = (2 - d) * 2 + u
        if (side, 2, u) in x_flights:
            x_flights[side, 2, u].wait_recv()
            total = total + x_in[side, u].astype(f32)
        x_out[side, slot] = total.astype(bf16)
        x_flights[side, d, u] = send(
            x_out.at[side, slot],
            x_in.at[side, slot],
            x_send.at[side * 4 + slot],
            x_recv.at[side * 4 + slot],
            at_x(1 - 2 * side),
        )

    for n in range(4):
        c_flights[n].wait_recv()
        labels[n] = labels[n] + c_in[n].astype(f32)
        if n == 0:
            x_step(0, 2, 0)
            x_step(1, 2, 1)
        if n == 2:
            x_step(0, 1, 1)
            x_step(1, 1, 0)

    pieces = []
    for u in range(SUBS):
        if u == SUBS - 1:
            x_step(0, 1, 0)
            x_step(1, 1, 1)
        for kind in range(2):
            ends = [(side, e) for side in range(2) for e in (1, 2) if NEXT[e] == 0]
            for side, e in ends:
                flights[kind, side, e, u].wait_recv()
            for s in range(u * PER, (u + 1) * PER):
                r = ROLL[s]
                b, q = place(kind, chunk_at(kind, 0), r)
                total = rows[b, q, :, kind * HALF : (kind + 1) * HALF]
                for side, e in ends:
                    total = total + ring_in[kind, side, 4 - e, s].astype(f32)
                if r == 0:
                    first_rows[kind, 0] = total
                    continue
                piece[kind, r] = total.astype(bf16)
                sem = kind * 8 + r
                pieces.append(
                    send(
                        piece.at[kind, r],
                        got.at[kind, r],
                        piece_send.at[sem],
                        piece_recv.at[sem],
                        at_y(r) if kind == 0 else at_z(r),
                    )
                )

    for u in range(2):
        part = slice(u * 64, (u + 1) * 64)
        x_flights[0, 1, u].wait_recv()
        x_flights[1, 1, u].wait_recv()
        label_ref[part] = (labels[3, part] + x_in[0, 2 + u].astype(f32) + x_in[1, 2 + u].astype(f32)).astype(bf16)

    for copy in pieces:
        copy.wait_recv()
    for kind in range(2):
        total = first_rows[kind, 0]
        for r in range(1, RING):
            total = total + got[kind, r].astype(f32)
        row_ref[:, kind * HALF : (kind + 1) * HALF] = total.astype(bf16)
    for copy in started:
        copy.wait_send()


def hand_over(row_in, label_in, row_ref, label_ref):
    row_ref[...] = row_in[...]
    label_ref[...] = label_in[...]


def on_device(embed, weight, bias, beam, positives):
    bf16, f32 = jnp.bfloat16, jnp.float32
    vmem = pl.BlockSpec(memory_space=pltpu.VMEM)
    hbm = pl.BlockSpec(memory_space=pltpu.HBM)
    dma = pltpu.SemaphoreType.DMA
    outs = (jax.ShapeDtypeStruct((16, 768), bf16), jax.ShapeDtypeStruct((128, 768), bf16))
    given = (embed.reshape(8, 8, 16, 768), weight, bias.reshape(8, 128), beam, positives.T)
    given = [pltpu.with_memory_space_constraint(array, pltpu.HBM) for array in given]
    found = pl.pallas_call(
        kernel,
        out_shape=outs,
        in_specs=[hbm] * 5,
        out_specs=(vmem, vmem),
        scratch_shapes=[
            pltpu.VMEM((8, 8, 16, 768), bf16),
            pltpu.VMEM((1024, 768), bf16),
            pltpu.VMEM((8, 128), bf16),
            pltpu.VMEM((8, 134), jnp.int32),
            pltpu.VMEM((8, 1024), jnp.int32),
            pltpu.VMEM((1024, 128), jnp.int32),
            pltpu.VMEM((8, 1024), f32),
            pltpu.VMEM((8, 8, 16, 1024), bf16),
            pltpu.VMEM((1024, 1024), bf16),
            pltpu.VMEM((8, 8, 16, 768), f32),
            pltpu.VMEM((4, 128, 768), f32),
            pltpu.VMEM((16, 16, 768), bf16),
            pltpu.VMEM((16, 16, 128), jnp.int32),
            pltpu.VMEM((16, 1024), f32),
            pltpu.VMEM((256, 1024), bf16),
            pltpu.VMEM((2, 8, 16, HALF), f32),
            pltpu.VMEM((2, 2, 4, 8, 16, HALF), bf16),
            pltpu.VMEM((2, 2, 4, 8, 16, HALF), bf16),
            pltpu.VMEM((2, 8, 16, HALF), bf16),
            pltpu.VMEM((2, 8, 16, HALF), bf16),
            pltpu.VMEM((4, 128, 768), bf16),
            pltpu.VMEM((4, 128, 768), bf16),
            pltpu.VMEM((2, 4, 64, 768), bf16),
            pltpu.VMEM((2, 4, 64, 768), bf16),
            dma((10,)),
            dma((16 * SUBS,)),
            dma((16 * SUBS,)),
            dma((16,)),
            dma((16,)),
            dma((4,)),
            dma((4,)),
            dma((8,)),
            dma((8,)),
        ],
        compiler_params=pltpu.CompilerParams(
            collective_id=0, has_side_effects=True, vmem_limit_bytes=40 * 1024 * 1024
        ),
        cost_estimate=pl.CostEstimate(
            flops=6 * 1024 * 1024 * 768, bytes_accessed=4 * 1024 * 1024, transcendentals=1024 * 1024
        ),
    )(*given)
    small = pltpu.CompilerParams(vmem_limit_bytes=2 * 1024 * 1024)
    return pl.pallas_call(hand_over, out_shape=outs, in_specs=[vmem, vmem], out_specs=(vmem, vmem), compiler_params=small)(*found)


def solution(mesh):
    in_specs = (P("dp", None), P("label", None), P("label"), P("dp", None), P("dp", None))
    out_specs = (P(("dp", "label"), None), P(("label", "dp"), None))
    return jax.shard_map(on_device, mesh=mesh, in_specs=in_specs, out_specs=out_specs, check_vma=False)
```

```python
import jax
import jax.numpy as jnp
from jax import lax
from jax.experimental import pallas as pl
from jax.experimental.pallas import tpu as pltpu
from jax.sharding import PartitionSpec as P

CLUSTER = 128
RING = 8
XRING = 4
HALF = 384
SUBS = 2
PER = RING // SUBS
NEXT = {4: 2, 3: 2, 2: 0, 1: 0}
ROLL = (4, 3, 5, 2, 6, 1, 7, 0)
NT = (((1,), (1,)), ((), ()))
MESH = pl.DeviceIdType.MESH


def mark_targets(pos_ref, marks, base):
    for blk in range(8):
        local = pos_ref[:, blk * 128 : (blk + 1) * 128] - base
        inside = (local >= 0) & (local < 1024)
        low = local & 127
        bit = jnp.where(inside, jnp.left_shift(1, (local >> 7) & 7), 0)
        lanes = lax.broadcasted_iota(jnp.int32, (128, 128), 0)
        found = jnp.zeros((128, 128), jnp.int32)
        for p in range(8):
            found = found | jnp.where(lanes == low[p : p + 1, :], bit[p : p + 1, :], 0)
        marks[blk * 128 : (blk + 1) * 128, :] = found.T


def scale_pairs(beam_ref, scale, first):
    beam = beam_ref[...]
    for j in range(8):
        hit = jnp.max(jnp.where(beam == first + j, 0.0625, 0.0), axis=1, keepdims=True)
        scale[:, j * 128 : (j + 1) * 128] = jnp.broadcast_to(hit, (8, 128))


def bend(scores, half_bias, marks, scale, j, groups):
    size = scores.shape[0] // groups
    bent = jnp.tanh(scores * 0.5 + half_bias[j : j + 1, :])
    sign = jnp.where((marks & (1 << j)) != 0, -1.0, 1.0)
    value = (bent + sign).reshape(groups, size, CLUSTER) * scale[:, None, :]
    return value.reshape(groups * size, CLUSTER)


def kernel(
    embed_hbm,
    weight_hbm,
    bias_hbm,
    beam_hbm,
    pos_hbm,
    row_ref,
    label_ref,
    embed,
    weight,
    bias_ref,
    beam_ref,
    pos_ref,
    marks,
    scale,
    slope,
    slope_t,
    rows,
    labels,
    first_embed,
    first_marks,
    first_scale,
    first_slope,
    first_rows,
    ring_out,
    ring_in,
    piece,
    got,
    c_out,
    c_in,
    x_out,
    x_in,
    load_sem,
    ring_send,
    ring_recv,
    piece_send,
    piece_recv,
    c_send,
    c_recv,
    x_send,
    x_recv,
):
    f32, bf16 = jnp.float32, jnp.bfloat16
    small = [
        pltpu.make_async_copy(pos_hbm, pos_ref, load_sem.at[5]),
        pltpu.make_async_copy(beam_hbm, beam_ref, load_sem.at[6]),
        pltpu.make_async_copy(bias_hbm, bias_ref, load_sem.at[7]),
    ]
    label = lax.axis_index("label")
    z, y = label // RING, label % RING
    loads = [
        pltpu.make_async_copy(embed_hbm.at[(z + 4) % RING], first_embed.at[0:8], load_sem.at[8]),
        pltpu.make_async_copy(embed_hbm.at[:, (y + 4) % RING], first_embed.at[8:16], load_sem.at[9]),
    ]
    loads += [
        pltpu.make_async_copy(weight_hbm.at[n * 256 : (n + 1) * 256], weight.at[n * 256 : (n + 1) * 256], load_sem.at[n])
        for n in range(4)
    ]
    whole = pltpu.make_async_copy(embed_hbm, embed, load_sem.at[4])
    for load in small + loads + [whole]:
        load.start()

    dp = lax.axis_index("dp")
    x, core = dp // 2, dp % 2

    def at_z(step):
        return (dp, ((z + step + RING) % RING) * RING + y)

    def at_y(step):
        return (dp, z * RING + (y + step + RING) % RING)

    def at_x(step):
        return (((x + step + XRING) % XRING) * 2 + core, label)

    sibling = (x * 2 + (1 - core), label)

    barrier = pltpu.get_barrier_semaphore()
    partners = [at_z(d) for d in range(1, 8)] + [at_y(d) for d in range(1, 8)] + [at_x(1), at_x(-1), sibling]
    for partner in partners:
        pl.semaphore_signal(barrier, inc=1, device_id=partner, device_id_type=MESH)

    for load in small:
        load.wait()
    scale_pairs(beam_ref, scale, label * 8)
    mark_targets(pos_ref, marks, label * 1024)
    half_bias = bias_ref[...].astype(f32) * 0.5

    def place(kind, chunk, r):
        return (chunk, (y + r) % RING) if kind == 0 else ((z + r) % RING, chunk)

    def chunk_at(kind, step):
        return ((z if kind == 0 else y) + step + RING) % RING

    for n in range(RING):
        for kind, b, q in ((0, (z + 4) % RING, n), (1, n, (y + 4) % RING)):
            first_marks[kind * 8 + n] = marks[pl.ds(pl.multiple_of(b * 128 + q * 16, 16), 16), :]
            first_scale[kind * 8 + n : kind * 8 + n + 1, :] = scale[pl.ds(b, 1), :]
    loads[0].wait()
    loads[1].wait()
    for nb in range(4):
        loads[2 + nb].wait()
        scores = lax.dot_general(
            first_embed[...].reshape(256, 768), weight[nb * 256 : (nb + 1) * 256, :], NT, preferred_element_type=f32
        )
        for h in range(2):
            j = 2 * nb + h
            cols = slice(j * 128, (j + 1) * 128)
            first_slope[:, cols] = bend(
                scores[:, h * 128 : (h + 1) * 128],
                half_bias,
                first_marks[...].reshape(256, 128),
                first_scale[:, cols],
                j,
                16,
            ).astype(bf16)
    for kind in range(2):
        first_rows[kind] = jnp.dot(
            first_slope[kind * 128 : (kind + 1) * 128, :],
            weight[:, kind * HALF : (kind + 1) * HALF],
            preferred_element_type=f32,
        ).reshape(8, 16, HALF)

    started = []

    def send(src, dst, send_sem, recv_sem, device):
        copy = pltpu.make_async_remote_copy(
            src_ref=src, dst_ref=dst, send_sem=send_sem, recv_sem=recv_sem, device_id=device, device_id_type=MESH
        )
        copy.start()
        started.append(copy)
        return copy

    flights = {}

    def is_long(side, u):
        return u // (SUBS // 2) == side

    def ring_step(kind, side, d, u):
        step = 1 if side == 0 else -1
        chunk = chunk_at(kind, step * d)
        slot = 4 - d
        before = [e for e in (4, 3, 2) if NEXT[e] == d and (e < 4 or is_long(side, u))]
        for e in before:
            flights[kind, side, e, u].wait_recv()
        for r in range(u * PER, (u + 1) * PER):
            b, q = place(kind, chunk, ROLL[r])
            if d == 4:
                total = first_rows[kind, q if kind == 0 else b]
            else:
                total = rows[b, q, :, kind * HALF : (kind + 1) * HALF]
            for e in before:
                total = total + ring_in[kind, side, 4 - e, r].astype(f32)
            ring_out[kind, side, slot, r] = total.astype(bf16)
        part = (kind, side, slot, slice(u * PER, (u + 1) * PER))
        sem = ((kind * 2 + side) * 4 + slot) * SUBS + u
        hops = step * (d - NEXT[d])
        flights[kind, side, d, u] = send(
            ring_out.at[part],
            ring_in.at[part],
            ring_send.at[sem],
            ring_recv.at[sem],
            at_z(hops) if kind == 0 else at_y(hops),
        )

    def wave(d, u):
        for side in range(2):
            for kind in range(2):
                if d < 4 or is_long(side, u):
                    ring_step(kind, side, d, u)

    def add_rows(steps, subs=SUBS, first=0):
        for kind in range(2):
            spots = [
                place(kind, chunk_at(kind, step), ROLL[r])
                for step in steps
                for r in range(first * PER, (first + subs) * PER)
            ]
            left = jnp.concatenate([slope[b, q] for b, q in spots], axis=0)
            cols = slice(kind * HALF, (kind + 1) * HALF)
            found = jnp.dot(left, weight[:, cols], preferred_element_type=f32)
            for n, (b, q) in enumerate(spots):
                rows[b, q, :, cols] = found[n * 16 : (n + 1) * 16]

    pl.semaphore_wait(barrier, len(partners))
    wave(4, 0)
    wave(4, 1)

    whole.wait()
    for nb in range(4):
        scores = lax.dot_general(
            embed[...].reshape(1024, 768), weight[nb * 256 : (nb + 1) * 256, :], NT, preferred_element_type=f32
        )
        for h in range(2):
            j = 2 * nb + h
            cols = slice(j * 128, (j + 1) * 128)
            value = bend(scores[:, h * 128 : (h + 1) * 128], half_bias, marks[...], scale[:, cols], j, 8)
            slope[:, :, :, cols] = value.astype(bf16).reshape(8, 8, 16, 128)
            slope_t[cols, :] = value.T.astype(bf16)
    add_rows((3, -3), 1, 0)
    wave(3, 0)
    add_rows((3, -3), 1, 1)
    wave(3, 1)
    add_rows((1, -1))
    wave(1, 0)
    wave(1, 1)

    order = [(x + 2) % XRING, (x + 1) % XRING, (x + 3) % XRING, x]

    def label_part(j):
        return jnp.dot(
            slope_t[pl.ds(pl.multiple_of(j * 128, 128), 128), :], embed[...].reshape(1024, 768), preferred_element_type=f32
        )

    c_flights = []
    for n, k in enumerate(order):
        c_out[n] = label_part(2 * k + 1 - core).astype(bf16)
        c_flights.append(send(c_out.at[n], c_in.at[n], c_send.at[n], c_recv.at[n], sibling))
    add_rows((2, -2))
    add_rows((0,))
    for n, k in enumerate(order):
        labels[n] = label_part(2 * k + core)
    wave(2, 0)
    wave(2, 1)

    x_flights = {}

    def x_step(side, d, u):
        n = 0 if d == 2 else 1 + side
        part = slice(u * 64, (u + 1) * 64)
        total = labels[n, part]
        slot = (2 - d) * 2 + u
        if (side, 2, u) in x_flights:
            x_flights[side, 2, u].wait_recv()
            total = total + x_in[side, u].astype(f32)
        x_out[side, slot] = total.astype(bf16)
        x_flights[side, d, u] = send(
            x_out.at[side, slot],
            x_in.at[side, slot],
            x_send.at[side * 4 + slot],
            x_recv.at[side * 4 + slot],
            at_x(1 - 2 * side),
        )

    for n in range(4):
        c_flights[n].wait_recv()
        labels[n] = labels[n] + c_in[n].astype(f32)
        if n == 0:
            x_step(0, 2, 0)
            x_step(1, 2, 1)
        if n == 2:
            x_step(0, 1, 1)
            x_step(1, 1, 0)

    pieces = []
    for u in range(SUBS):
        if u == SUBS - 1:
            x_step(0, 1, 0)
            x_step(1, 1, 1)
        for kind in range(2):
            ends = [(side, e) for side in range(2) for e in (1, 2) if NEXT[e] == 0]
            for side, e in ends:
                flights[kind, side, e, u].wait_recv()
            for s in range(u * PER, (u + 1) * PER):
                r = ROLL[s]
                b, q = place(kind, chunk_at(kind, 0), r)
                total = rows[b, q, :, kind * HALF : (kind + 1) * HALF]
                for side, e in ends:
                    total = total + ring_in[kind, side, 4 - e, s].astype(f32)
                if r == 0:
                    first_rows[kind, 0] = total
                    continue
                piece[kind, r] = total.astype(bf16)
                sem = kind * 8 + r
                pieces.append(
                    send(
                        piece.at[kind, r],
                        got.at[kind, r],
                        piece_send.at[sem],
                        piece_recv.at[sem],
                        at_y(r) if kind == 0 else at_z(r),
                    )
                )

    for u in range(2):
        part = slice(u * 64, (u + 1) * 64)
        x_flights[0, 1, u].wait_recv()
        x_flights[1, 1, u].wait_recv()
        label_ref[part] = (labels[3, part] + x_in[0, 2 + u].astype(f32) + x_in[1, 2 + u].astype(f32)).astype(bf16)

    for copy in pieces:
        copy.wait_recv()
    for kind in range(2):
        total = first_rows[kind, 0]
        for r in range(1, RING):
            total = total + got[kind, r].astype(f32)
        row_ref[:, kind * HALF : (kind + 1) * HALF] = total.astype(bf16)
    for copy in started:
        copy.wait_send()


def hand_over(row_in, label_in, row_ref, label_ref):
    row_ref[...] = row_in[...]
    label_ref[...] = label_in[...]


def on_device(embed, weight, bias, beam, positives):
    bf16, f32 = jnp.bfloat16, jnp.float32
    vmem = pl.BlockSpec(memory_space=pltpu.VMEM)
    hbm = pl.BlockSpec(memory_space=pltpu.HBM)
    dma = pltpu.SemaphoreType.DMA
    outs = (jax.ShapeDtypeStruct((16, 768), bf16), jax.ShapeDtypeStruct((128, 768), bf16))
    given = (embed.reshape(8, 8, 16, 768), weight, bias.reshape(8, 128), beam, positives.T)
    given = [pltpu.with_memory_space_constraint(array, pltpu.HBM) for array in given]
    found = pl.pallas_call(
        kernel,
        out_shape=outs,
        in_specs=[hbm] * 5,
        out_specs=(vmem, vmem),
        scratch_shapes=[
            pltpu.VMEM((8, 8, 16, 768), bf16),
            pltpu.VMEM((1024, 768), bf16),
            pltpu.VMEM((8, 128), bf16),
            pltpu.VMEM((8, 134), jnp.int32),
            pltpu.VMEM((8, 1024), jnp.int32),
            pltpu.VMEM((1024, 128), jnp.int32),
            pltpu.VMEM((8, 1024), f32),
            pltpu.VMEM((8, 8, 16, 1024), bf16),
            pltpu.VMEM((1024, 1024), bf16),
            pltpu.VMEM((8, 8, 16, 768), f32),
            pltpu.VMEM((4, 128, 768), f32),
            pltpu.VMEM((16, 16, 768), bf16),
            pltpu.VMEM((16, 16, 128), jnp.int32),
            pltpu.VMEM((16, 1024), f32),
            pltpu.VMEM((256, 1024), bf16),
            pltpu.VMEM((2, 8, 16, HALF), f32),
            pltpu.VMEM((2, 2, 4, 8, 16, HALF), bf16),
            pltpu.VMEM((2, 2, 4, 8, 16, HALF), bf16),
            pltpu.VMEM((2, 8, 16, HALF), bf16),
            pltpu.VMEM((2, 8, 16, HALF), bf16),
            pltpu.VMEM((4, 128, 768), bf16),
            pltpu.VMEM((4, 128, 768), bf16),
            pltpu.VMEM((2, 4, 64, 768), bf16),
            pltpu.VMEM((2, 4, 64, 768), bf16),
            dma((10,)),
            dma((16 * SUBS,)),
            dma((16 * SUBS,)),
            dma((16,)),
            dma((16,)),
            dma((4,)),
            dma((4,)),
            dma((8,)),
            dma((8,)),
        ],
        compiler_params=pltpu.CompilerParams(
            collective_id=0, has_side_effects=True, vmem_limit_bytes=40 * 1024 * 1024
        ),
        cost_estimate=pl.CostEstimate(
            flops=6 * 1024 * 1024 * 768, bytes_accessed=4 * 1024 * 1024, transcendentals=1024 * 1024
        ),
    )(*given)
    small = pltpu.CompilerParams(vmem_limit_bytes=2 * 1024 * 1024)
    return pl.pallas_call(hand_over, out_shape=outs, in_specs=[vmem, vmem], out_specs=(vmem, vmem), compiler_params=small)(*found)


def solution(mesh):
    in_specs = (P("dp", None), P("label", None), P("label"), P("dp", None), P("dp", None))
    out_specs = (P(("dp", "label"), None), P(("label", "dp"), None))
    return jax.shard_map(on_device, mesh=mesh, in_specs=in_specs, out_specs=out_specs, check_vma=False)
```

```python
import jax
import jax.numpy as jnp
from jax import lax
from jax.experimental import pallas as pl
from jax.experimental.pallas import tpu as pltpu
from jax.sharding import PartitionSpec as P

CLUSTER = 128
RING = 8
XRING = 4
HALF = 384
SUBS = 2
PER = RING // SUBS
NEXT = {4: 2, 3: 2, 2: 0, 1: 0}
ROLL = (4, 3, 5, 2, 6, 1, 7, 0)
NT = (((1,), (1,)), ((), ()))
MESH = pl.DeviceIdType.MESH


def mark_targets(pos_ref, marks, base):
    for blk in range(8):
        local = pos_ref[:, blk * 128 : (blk + 1) * 128] - base
        inside = (local >= 0) & (local < 1024)
        low = local & 127
        bit = jnp.where(inside, jnp.left_shift(1, (local >> 7) & 7), 0)
        lanes = lax.broadcasted_iota(jnp.int32, (128, 128), 0)
        found = jnp.zeros((128, 128), jnp.int32)
        for p in range(8):
            found = found | jnp.where(lanes == low[p : p + 1, :], bit[p : p + 1, :], 0)
        marks[blk * 128 : (blk + 1) * 128, :] = found.T


def scale_pairs(beam_ref, scale, first):
    beam = beam_ref[...]
    for j in range(8):
        hit = jnp.max(jnp.where(beam == first + j, 0.0625, 0.0), axis=1, keepdims=True)
        scale[:, j * 128 : (j + 1) * 128] = jnp.broadcast_to(hit, (8, 128))


def bend(scores, half_bias, marks, scale, j, groups):
    size = scores.shape[0] // groups
    bent = jnp.tanh(scores * 0.5 + half_bias[j : j + 1, :])
    sign = jnp.where((marks & (1 << j)) != 0, -1.0, 1.0)
    value = (bent + sign).reshape(groups, size, CLUSTER) * scale[:, None, :]
    return value.reshape(groups * size, CLUSTER)


def kernel(
    embed_hbm,
    weight_hbm,
    bias_hbm,
    beam_hbm,
    pos_hbm,
    row_ref,
    label_ref,
    embed,
    weight,
    bias_ref,
    beam_ref,
    pos_ref,
    marks,
    scale,
    slope,
    slope_t,
    rows,
    labels,
    first_embed,
    first_marks,
    first_scale,
    first_slope,
    first_rows,
    ring_out,
    ring_in,
    piece,
    got,
    c_out,
    c_in,
    x_out,
    x_in,
    load_sem,
    ring_send,
    ring_recv,
    piece_send,
    piece_recv,
    c_send,
    c_recv,
    x_send,
    x_recv,
):
    f32, bf16 = jnp.float32, jnp.bfloat16
    small = [
        pltpu.make_async_copy(pos_hbm, pos_ref, load_sem.at[5]),
        pltpu.make_async_copy(beam_hbm, beam_ref, load_sem.at[6]),
        pltpu.make_async_copy(bias_hbm, bias_ref, load_sem.at[7]),
    ]
    label = lax.axis_index("label")
    z, y = label // RING, label % RING
    loads = [
        pltpu.make_async_copy(embed_hbm.at[(z + 4) % RING], first_embed.at[0:8], load_sem.at[8]),
        pltpu.make_async_copy(embed_hbm.at[:, (y + 4) % RING], first_embed.at[8:16], load_sem.at[9]),
    ]
    loads += [
        pltpu.make_async_copy(weight_hbm.at[n * 256 : (n + 1) * 256], weight.at[n * 256 : (n + 1) * 256], load_sem.at[n])
        for n in range(4)
    ]
    whole = pltpu.make_async_copy(embed_hbm, embed, load_sem.at[4])
    for load in small + loads + [whole]:
        load.start()

    dp = lax.axis_index("dp")
    x, core = dp // 2, dp % 2

    def at_z(step):
        return (dp, ((z + step + RING) % RING) * RING + y)

    def at_y(step):
        return (dp, z * RING + (y + step + RING) % RING)

    def at_x(step):
        return (((x + step + XRING) % XRING) * 2 + core, label)

    sibling = (x * 2 + (1 - core), label)

    barrier = pltpu.get_barrier_semaphore()
    partners = [at_z(d) for d in range(1, 8)] + [at_y(d) for d in range(1, 8)] + [at_x(1), at_x(-1), sibling]
    for partner in partners:
        pl.semaphore_signal(barrier, inc=1, device_id=partner, device_id_type=MESH)

    for load in small:
        load.wait()
    scale_pairs(beam_ref, scale, label * 8)
    mark_targets(pos_ref, marks, label * 1024)
    half_bias = bias_ref[...].astype(f32) * 0.5

    def place(kind, chunk, r):
        return (chunk, (y + r) % RING) if kind == 0 else ((z + r) % RING, chunk)

    def chunk_at(kind, step):
        return ((z if kind == 0 else y) + step + RING) % RING

    for n in range(RING):
        for kind, b, q in ((0, (z + 4) % RING, n), (1, n, (y + 4) % RING)):
            first_marks[kind * 8 + n] = marks[pl.ds(pl.multiple_of(b * 128 + q * 16, 16), 16), :]
            first_scale[kind * 8 + n : kind * 8 + n + 1, :] = scale[pl.ds(b, 1), :]
    loads[0].wait()
    loads[1].wait()
    for nb in range(4):
        loads[2 + nb].wait()
        scores = lax.dot_general(
            first_embed[...].reshape(256, 768), weight[nb * 256 : (nb + 1) * 256, :], NT, preferred_element_type=f32
        )
        for h in range(2):
            j = 2 * nb + h
            cols = slice(j * 128, (j + 1) * 128)
            first_slope[:, cols] = bend(
                scores[:, h * 128 : (h + 1) * 128],
                half_bias,
                first_marks[...].reshape(256, 128),
                first_scale[:, cols],
                j,
                16,
            ).astype(bf16)
    for kind in range(2):
        first_rows[kind] = jnp.dot(
            first_slope[kind * 128 : (kind + 1) * 128, :],
            weight[:, kind * HALF : (kind + 1) * HALF],
            preferred_element_type=f32,
        ).reshape(8, 16, HALF)

    started = []

    def send(src, dst, send_sem, recv_sem, device):
        copy = pltpu.make_async_remote_copy(
            src_ref=src, dst_ref=dst, send_sem=send_sem, recv_sem=recv_sem, device_id=device, device_id_type=MESH
        )
        copy.start()
        started.append(copy)
        return copy

    flights = {}

    def is_long(side, u):
        return u // (SUBS // 2) == side

    def ring_step(kind, side, d, u):
        step = 1 if side == 0 else -1
        chunk = chunk_at(kind, step * d)
        slot = 4 - d
        before = [e for e in (4, 3, 2) if NEXT[e] == d and (e < 4 or is_long(side, u))]
        for e in before:
            flights[kind, side, e, u].wait_recv()
        for r in range(u * PER, (u + 1) * PER):
            b, q = place(kind, chunk, ROLL[r])
            if d == 4:
                total = first_rows[kind, q if kind == 0 else b]
            else:
                total = rows[b, q, :, kind * HALF : (kind + 1) * HALF]
            for e in before:
                total = total + ring_in[kind, side, 4 - e, r].astype(f32)
            ring_out[kind, side, slot, r] = total.astype(bf16)
        part = (kind, side, slot, slice(u * PER, (u + 1) * PER))
        sem = ((kind * 2 + side) * 4 + slot) * SUBS + u
        hops = step * (d - NEXT[d])
        flights[kind, side, d, u] = send(
            ring_out.at[part],
            ring_in.at[part],
            ring_send.at[sem],
            ring_recv.at[sem],
            at_z(hops) if kind == 0 else at_y(hops),
        )

    def wave(d, u):
        for side in range(2):
            for kind in range(2):
                if d < 4 or is_long(side, u):
                    ring_step(kind, side, d, u)

    def add_rows(steps, subs=SUBS, first=0):
        for kind in range(2):
            spots = [
                place(kind, chunk_at(kind, step), ROLL[r])
                for step in steps
                for r in range(first * PER, (first + subs) * PER)
            ]
            left = jnp.concatenate([slope[b, q] for b, q in spots], axis=0)
            cols = slice(kind * HALF, (kind + 1) * HALF)
            found = jnp.dot(left, weight[:, cols], preferred_element_type=f32)
            for n, (b, q) in enumerate(spots):
                rows[b, q, :, cols] = found[n * 16 : (n + 1) * 16]

    pl.semaphore_wait(barrier, len(partners))
    wave(4, 0)
    wave(4, 1)

    whole.wait()
    for nb in range(4):
        scores = lax.dot_general(
            embed[...].reshape(1024, 768), weight[nb * 256 : (nb + 1) * 256, :], NT, preferred_element_type=f32
        )
        for h in range(2):
            j = 2 * nb + h
            cols = slice(j * 128, (j + 1) * 128)
            value = bend(scores[:, h * 128 : (h + 1) * 128], half_bias, marks[...], scale[:, cols], j, 8)
            slope[:, :, :, cols] = value.astype(bf16).reshape(8, 8, 16, 128)
            slope_t[cols, :] = value.T.astype(bf16)
    add_rows((3, -3), 1, 0)
    wave(3, 0)
    add_rows((3, -3), 1, 1)
    wave(3, 1)
    add_rows((1, -1))
    wave(1, 0)
    wave(1, 1)

    order = [(x + 2) % XRING, (x + 1) % XRING, (x + 3) % XRING, x]

    def label_part(j):
        return jnp.dot(
            slope_t[pl.ds(pl.multiple_of(j * 128, 128), 128), :], embed[...].reshape(1024, 768), preferred_element_type=f32
        )

    c_flights = []
    for n, k in enumerate(order):
        c_out[n] = label_part(2 * k + 1 - core).astype(bf16)
        c_flights.append(send(c_out.at[n], c_in.at[n], c_send.at[n], c_recv.at[n], sibling))
    add_rows((2, -2))
    add_rows((0,))
    for n, k in enumerate(order):
        labels[n] = label_part(2 * k + core)
    wave(2, 0)
    wave(2, 1)

    x_flights = {}

    def x_step(side, d, u):
        n = 0 if d == 2 else 1 + side
        part = slice(u * 64, (u + 1) * 64)
        total = labels[n, part]
        slot = (2 - d) * 2 + u
        if (side, 2, u) in x_flights:
            x_flights[side, 2, u].wait_recv()
            total = total + x_in[side, u].astype(f32)
        x_out[side, slot] = total.astype(bf16)
        x_flights[side, d, u] = send(
            x_out.at[side, slot],
            x_in.at[side, slot],
            x_send.at[side * 4 + slot],
            x_recv.at[side * 4 + slot],
            at_x(1 - 2 * side),
        )

    for n in range(4):
        c_flights[n].wait_recv()
        labels[n] = labels[n] + c_in[n].astype(f32)
        if n == 0:
            x_step(0, 2, 0)
            x_step(1, 2, 1)
        if n == 2:
            x_step(0, 1, 1)
            x_step(1, 1, 0)

    x_step(0, 1, 0)
    x_step(1, 1, 1)
    pieces = []
    for u in range(SUBS):
        for kind in range(2):
            ends = [(side, e) for side in range(2) for e in (1, 2) if NEXT[e] == 0]
            for side, e in ends:
                flights[kind, side, e, u].wait_recv()
            for s in range(u * PER, (u + 1) * PER):
                r = ROLL[s]
                b, q = place(kind, chunk_at(kind, 0), r)
                total = rows[b, q, :, kind * HALF : (kind + 1) * HALF]
                for side, e in ends:
                    total = total + ring_in[kind, side, 4 - e, s].astype(f32)
                if r == 0:
                    first_rows[kind, 0] = total
                    continue
                piece[kind, r] = total.astype(bf16)
                sem = kind * 8 + r
                pieces.append(
                    send(
                        piece.at[kind, r],
                        got.at[kind, r],
                        piece_send.at[sem],
                        piece_recv.at[sem],
                        at_y(r) if kind == 0 else at_z(r),
                    )
                )

    for u in range(2):
        part = slice(u * 64, (u + 1) * 64)
        x_flights[0, 1, u].wait_recv()
        x_flights[1, 1, u].wait_recv()
        label_ref[part] = (labels[3, part] + x_in[0, 2 + u].astype(f32) + x_in[1, 2 + u].astype(f32)).astype(bf16)

    for copy in pieces:
        copy.wait_recv()
    for kind in range(2):
        total = first_rows[kind, 0]
        for r in range(1, RING):
            total = total + got[kind, r].astype(f32)
        row_ref[:, kind * HALF : (kind + 1) * HALF] = total.astype(bf16)
    for copy in started:
        copy.wait_send()


def hand_over(row_in, label_in, row_ref, label_ref):
    row_ref[...] = row_in[...]
    label_ref[...] = label_in[...]


def on_device(embed, weight, bias, beam, positives):
    bf16, f32 = jnp.bfloat16, jnp.float32
    vmem = pl.BlockSpec(memory_space=pltpu.VMEM)
    hbm = pl.BlockSpec(memory_space=pltpu.HBM)
    dma = pltpu.SemaphoreType.DMA
    outs = (jax.ShapeDtypeStruct((16, 768), bf16), jax.ShapeDtypeStruct((128, 768), bf16))
    given = (embed.reshape(8, 8, 16, 768), weight, bias.reshape(8, 128), beam, positives.T)
    given = [pltpu.with_memory_space_constraint(array, pltpu.HBM) for array in given]
    found = pl.pallas_call(
        kernel,
        out_shape=outs,
        in_specs=[hbm] * 5,
        out_specs=(vmem, vmem),
        scratch_shapes=[
            pltpu.VMEM((8, 8, 16, 768), bf16),
            pltpu.VMEM((1024, 768), bf16),
            pltpu.VMEM((8, 128), bf16),
            pltpu.VMEM((8, 134), jnp.int32),
            pltpu.VMEM((8, 1024), jnp.int32),
            pltpu.VMEM((1024, 128), jnp.int32),
            pltpu.VMEM((8, 1024), f32),
            pltpu.VMEM((8, 8, 16, 1024), bf16),
            pltpu.VMEM((1024, 1024), bf16),
            pltpu.VMEM((8, 8, 16, 768), f32),
            pltpu.VMEM((4, 128, 768), f32),
            pltpu.VMEM((16, 16, 768), bf16),
            pltpu.VMEM((16, 16, 128), jnp.int32),
            pltpu.VMEM((16, 1024), f32),
            pltpu.VMEM((256, 1024), bf16),
            pltpu.VMEM((2, 8, 16, HALF), f32),
            pltpu.VMEM((2, 2, 4, 8, 16, HALF), bf16),
            pltpu.VMEM((2, 2, 4, 8, 16, HALF), bf16),
            pltpu.VMEM((2, 8, 16, HALF), bf16),
            pltpu.VMEM((2, 8, 16, HALF), bf16),
            pltpu.VMEM((4, 128, 768), bf16),
            pltpu.VMEM((4, 128, 768), bf16),
            pltpu.VMEM((2, 4, 64, 768), bf16),
            pltpu.VMEM((2, 4, 64, 768), bf16),
            dma((10,)),
            dma((16 * SUBS,)),
            dma((16 * SUBS,)),
            dma((16,)),
            dma((16,)),
            dma((4,)),
            dma((4,)),
            dma((8,)),
            dma((8,)),
        ],
        compiler_params=pltpu.CompilerParams(
            collective_id=0, has_side_effects=True, vmem_limit_bytes=40 * 1024 * 1024
        ),
        cost_estimate=pl.CostEstimate(
            flops=6 * 1024 * 1024 * 768, bytes_accessed=4 * 1024 * 1024, transcendentals=1024 * 1024
        ),
    )(*given)
    small = pltpu.CompilerParams(vmem_limit_bytes=2 * 1024 * 1024)
    return pl.pallas_call(hand_over, out_shape=outs, in_specs=[vmem, vmem], out_specs=(vmem, vmem), compiler_params=small)(*found)


def solution(mesh):
    in_specs = (P("dp", None), P("label", None), P("label"), P("dp", None), P("dp", None))
    out_specs = (P(("dp", "label"), None), P(("label", "dp"), None))
    return jax.shard_map(on_device, mesh=mesh, in_specs=in_specs, out_specs=out_specs, check_vma=False)
```

```python
import jax
import jax.numpy as jnp
from jax import lax
from jax.experimental import pallas as pl
from jax.experimental.pallas import tpu as pltpu
from jax.sharding import PartitionSpec as P

CLUSTER = 128
RING = 8
XRING = 4
HALF = 384
SUBS = 2
PER = RING // SUBS
NEXT = {4: 2, 3: 2, 2: 0, 1: 0}
ROLL = (4, 3, 5, 2, 6, 1, 7, 0)
NT = (((1,), (1,)), ((), ()))
MESH = pl.DeviceIdType.MESH


def mark_targets(pos_ref, marks, base):
    for blk in range(8):
        local = pos_ref[:, blk * 128 : (blk + 1) * 128] - base
        inside = (local >= 0) & (local < 1024)
        low = local & 127
        bit = jnp.where(inside, jnp.left_shift(1, (local >> 7) & 7), 0)
        lanes = lax.broadcasted_iota(jnp.int32, (128, 128), 0)
        found = jnp.zeros((128, 128), jnp.int32)
        for p in range(8):
            found = found | jnp.where(lanes == low[p : p + 1, :], bit[p : p + 1, :], 0)
        marks[blk * 128 : (blk + 1) * 128, :] = found.T


def scale_pairs(beam_ref, scale, first):
    beam = beam_ref[...]
    for j in range(8):
        hit = jnp.max(jnp.where(beam == first + j, 0.0625, 0.0), axis=1, keepdims=True)
        scale[:, j * 128 : (j + 1) * 128] = jnp.broadcast_to(hit, (8, 128))


def bend(scores, half_bias, marks, scale, j, groups):
    size = scores.shape[0] // groups
    bent = jnp.tanh(scores * 0.5 + half_bias[j : j + 1, :])
    sign = jnp.where((marks & (1 << j)) != 0, -1.0, 1.0)
    value = (bent + sign).reshape(groups, size, CLUSTER) * scale[:, None, :]
    return value.reshape(groups * size, CLUSTER)


def kernel(
    embed_hbm,
    weight_hbm,
    bias_hbm,
    beam_hbm,
    pos_hbm,
    row_ref,
    label_ref,
    embed,
    weight,
    bias_ref,
    beam_ref,
    pos_ref,
    marks,
    scale,
    slope,
    slope_t,
    rows,
    labels,
    first_embed,
    first_marks,
    first_scale,
    first_scores,
    first_slope,
    first_rows,
    ring_out,
    ring_in,
    piece,
    got,
    c_out,
    c_in,
    x_out,
    x_in,
    load_sem,
    ring_send,
    ring_recv,
    piece_send,
    piece_recv,
    c_send,
    c_recv,
    x_send,
    x_recv,
):
    f32, bf16 = jnp.float32, jnp.bfloat16
    small = [
        pltpu.make_async_copy(pos_hbm, pos_ref, load_sem.at[5]),
        pltpu.make_async_copy(beam_hbm, beam_ref, load_sem.at[6]),
        pltpu.make_async_copy(bias_hbm, bias_ref, load_sem.at[7]),
    ]
    label = lax.axis_index("label")
    z, y = label // RING, label % RING
    loads = [
        pltpu.make_async_copy(embed_hbm.at[(z + 4) % RING], first_embed.at[0:8], load_sem.at[8]),
        pltpu.make_async_copy(embed_hbm.at[:, (y + 4) % RING], first_embed.at[8:16], load_sem.at[9]),
    ]
    loads += [
        pltpu.make_async_copy(weight_hbm.at[n * 256 : (n + 1) * 256], weight.at[n * 256 : (n + 1) * 256], load_sem.at[n])
        for n in range(4)
    ]
    whole = pltpu.make_async_copy(embed_hbm, embed, load_sem.at[4])
    for load in small + loads + [whole]:
        load.start()

    dp = lax.axis_index("dp")
    x, core = dp // 2, dp % 2

    def at_z(step):
        return (dp, ((z + step + RING) % RING) * RING + y)

    def at_y(step):
        return (dp, z * RING + (y + step + RING) % RING)

    def at_x(step):
        return (((x + step + XRING) % XRING) * 2 + core, label)

    sibling = (x * 2 + (1 - core), label)

    barrier = pltpu.get_barrier_semaphore()
    partners = [at_z(d) for d in range(1, 8)] + [at_y(d) for d in range(1, 8)] + [at_x(1), at_x(-1), sibling]
    for partner in partners:
        pl.semaphore_signal(barrier, inc=1, device_id=partner, device_id_type=MESH)


    def place(kind, chunk, r):
        return (chunk, (y + r) % RING) if kind == 0 else ((z + r) % RING, chunk)

    def chunk_at(kind, step):
        return ((z if kind == 0 else y) + step + RING) % RING

    loads[0].wait()
    loads[1].wait()
    for nb in range(4):
        loads[2 + nb].wait()
        first_scores[:, nb * 256 : (nb + 1) * 256] = lax.dot_general(
            first_embed[...].reshape(256, 768), weight[nb * 256 : (nb + 1) * 256, :], NT, preferred_element_type=f32
        )
    for load in small:
        load.wait()
    scale_pairs(beam_ref, scale, label * 8)
    mark_targets(pos_ref, marks, label * 1024)
    half_bias = bias_ref[...].astype(f32) * 0.5
    for n in range(RING):
        for kind, b, q in ((0, (z + 4) % RING, n), (1, n, (y + 4) % RING)):
            first_marks[kind * 8 + n] = marks[pl.ds(pl.multiple_of(b * 128 + q * 16, 16), 16), :]
            first_scale[kind * 8 + n : kind * 8 + n + 1, :] = scale[pl.ds(b, 1), :]
    for j in range(8):
        cols = slice(j * 128, (j + 1) * 128)
        first_slope[:, cols] = bend(
            first_scores[:, cols], half_bias, first_marks[...].reshape(256, 128), first_scale[:, cols], j, 16
        ).astype(bf16)
    for kind in range(2):
        first_rows[kind] = jnp.dot(
            first_slope[kind * 128 : (kind + 1) * 128, :],
            weight[:, kind * HALF : (kind + 1) * HALF],
            preferred_element_type=f32,
        ).reshape(8, 16, HALF)

    started = []

    def send(src, dst, send_sem, recv_sem, device):
        copy = pltpu.make_async_remote_copy(
            src_ref=src, dst_ref=dst, send_sem=send_sem, recv_sem=recv_sem, device_id=device, device_id_type=MESH
        )
        copy.start()
        started.append(copy)
        return copy

    flights = {}

    def is_long(side, u):
        return u // (SUBS // 2) == side

    def ring_step(kind, side, d, u):
        step = 1 if side == 0 else -1
        chunk = chunk_at(kind, step * d)
        slot = 4 - d
        before = [e for e in (4, 3, 2) if NEXT[e] == d and (e < 4 or is_long(side, u))]
        for e in before:
            flights[kind, side, e, u].wait_recv()
        for r in range(u * PER, (u + 1) * PER):
            b, q = place(kind, chunk, ROLL[r])
            if d == 4:
                total = first_rows[kind, q if kind == 0 else b]
            else:
                total = rows[b, q, :, kind * HALF : (kind + 1) * HALF]
            for e in before:
                total = total + ring_in[kind, side, 4 - e, r].astype(f32)
            ring_out[kind, side, slot, r] = total.astype(bf16)
        part = (kind, side, slot, slice(u * PER, (u + 1) * PER))
        sem = ((kind * 2 + side) * 4 + slot) * SUBS + u
        hops = step * (d - NEXT[d])
        flights[kind, side, d, u] = send(
            ring_out.at[part],
            ring_in.at[part],
            ring_send.at[sem],
            ring_recv.at[sem],
            at_z(hops) if kind == 0 else at_y(hops),
        )

    def wave(d, u):
        for side in range(2):
            for kind in range(2):
                if d < 4 or is_long(side, u):
                    ring_step(kind, side, d, u)

    def add_rows(steps, subs=SUBS, first=0):
        for kind in range(2):
            spots = [
                place(kind, chunk_at(kind, step), ROLL[r])
                for step in steps
                for r in range(first * PER, (first + subs) * PER)
            ]
            left = jnp.concatenate([slope[b, q] for b, q in spots], axis=0)
            cols = slice(kind * HALF, (kind + 1) * HALF)
            found = jnp.dot(left, weight[:, cols], preferred_element_type=f32)
            for n, (b, q) in enumerate(spots):
                rows[b, q, :, cols] = found[n * 16 : (n + 1) * 16]

    pl.semaphore_wait(barrier, len(partners))
    wave(4, 0)
    wave(4, 1)

    whole.wait()
    for nb in range(4):
        scores = lax.dot_general(
            embed[...].reshape(1024, 768), weight[nb * 256 : (nb + 1) * 256, :], NT, preferred_element_type=f32
        )
        for h in range(2):
            j = 2 * nb + h
            cols = slice(j * 128, (j + 1) * 128)
            value = bend(scores[:, h * 128 : (h + 1) * 128], half_bias, marks[...], scale[:, cols], j, 8)
            slope[:, :, :, cols] = value.astype(bf16).reshape(8, 8, 16, 128)
            slope_t[cols, :] = value.T.astype(bf16)
    add_rows((3, -3), 1, 0)
    wave(3, 0)
    add_rows((3, -3), 1, 1)
    wave(3, 1)
    add_rows((1, -1))
    wave(1, 0)
    wave(1, 1)

    order = [(x + 2) % XRING, (x + 1) % XRING, (x + 3) % XRING, x]

    def label_part(j):
        return jnp.dot(
            slope_t[pl.ds(pl.multiple_of(j * 128, 128), 128), :], embed[...].reshape(1024, 768), preferred_element_type=f32
        )

    c_flights = []
    for n, k in enumerate(order):
        c_out[n] = label_part(2 * k + 1 - core).astype(bf16)
        c_flights.append(send(c_out.at[n], c_in.at[n], c_send.at[n], c_recv.at[n], sibling))
    add_rows((2, -2))
    add_rows((0,))
    for n, k in enumerate(order):
        labels[n] = label_part(2 * k + core)
    wave(2, 0)
    wave(2, 1)

    x_flights = {}

    def x_step(side, d, u):
        n = 0 if d == 2 else 1 + side
        part = slice(u * 64, (u + 1) * 64)
        total = labels[n, part]
        slot = (2 - d) * 2 + u
        if (side, 2, u) in x_flights:
            x_flights[side, 2, u].wait_recv()
            total = total + x_in[side, u].astype(f32)
        x_out[side, slot] = total.astype(bf16)
        x_flights[side, d, u] = send(
            x_out.at[side, slot],
            x_in.at[side, slot],
            x_send.at[side * 4 + slot],
            x_recv.at[side * 4 + slot],
            at_x(1 - 2 * side),
        )

    for n in range(4):
        c_flights[n].wait_recv()
        labels[n] = labels[n] + c_in[n].astype(f32)
        if n == 0:
            x_step(0, 2, 0)
            x_step(1, 2, 1)
        if n == 2:
            x_step(0, 1, 1)
            x_step(1, 1, 0)

    x_step(0, 1, 0)
    x_step(1, 1, 1)
    pieces = []
    for u in range(SUBS):
        for kind in range(2):
            ends = [(side, e) for side in range(2) for e in (1, 2) if NEXT[e] == 0]
            for side, e in ends:
                flights[kind, side, e, u].wait_recv()
            for s in range(u * PER, (u + 1) * PER):
                r = ROLL[s]
                b, q = place(kind, chunk_at(kind, 0), r)
                total = rows[b, q, :, kind * HALF : (kind + 1) * HALF]
                for side, e in ends:
                    total = total + ring_in[kind, side, 4 - e, s].astype(f32)
                if r == 0:
                    first_rows[kind, 0] = total
                    continue
                piece[kind, r] = total.astype(bf16)
                sem = kind * 8 + r
                pieces.append(
                    send(
                        piece.at[kind, r],
                        got.at[kind, r],
                        piece_send.at[sem],
                        piece_recv.at[sem],
                        at_y(r) if kind == 0 else at_z(r),
                    )
                )

    for u in range(2):
        part = slice(u * 64, (u + 1) * 64)
        x_flights[0, 1, u].wait_recv()
        x_flights[1, 1, u].wait_recv()
        label_ref[part] = (labels[3, part] + x_in[0, 2 + u].astype(f32) + x_in[1, 2 + u].astype(f32)).astype(bf16)

    for copy in pieces:
        copy.wait_recv()
    for kind in range(2):
        total = first_rows[kind, 0]
        for r in range(1, RING):
            total = total + got[kind, r].astype(f32)
        row_ref[:, kind * HALF : (kind + 1) * HALF] = total.astype(bf16)
    for copy in started:
        copy.wait_send()


def hand_over(row_in, label_in, row_ref, label_ref):
    row_ref[...] = row_in[...]
    label_ref[...] = label_in[...]


def on_device(embed, weight, bias, beam, positives):
    bf16, f32 = jnp.bfloat16, jnp.float32
    vmem = pl.BlockSpec(memory_space=pltpu.VMEM)
    hbm = pl.BlockSpec(memory_space=pltpu.HBM)
    dma = pltpu.SemaphoreType.DMA
    outs = (jax.ShapeDtypeStruct((16, 768), bf16), jax.ShapeDtypeStruct((128, 768), bf16))
    given = (embed.reshape(8, 8, 16, 768), weight, bias.reshape(8, 128), beam, positives.T)
    given = [pltpu.with_memory_space_constraint(array, pltpu.HBM) for array in given]
    found = pl.pallas_call(
        kernel,
        out_shape=outs,
        in_specs=[hbm] * 5,
        out_specs=(vmem, vmem),
        scratch_shapes=[
            pltpu.VMEM((8, 8, 16, 768), bf16),
            pltpu.VMEM((1024, 768), bf16),
            pltpu.VMEM((8, 128), bf16),
            pltpu.VMEM((8, 134), jnp.int32),
            pltpu.VMEM((8, 1024), jnp.int32),
            pltpu.VMEM((1024, 128), jnp.int32),
            pltpu.VMEM((8, 1024), f32),
            pltpu.VMEM((8, 8, 16, 1024), bf16),
            pltpu.VMEM((1024, 1024), bf16),
            pltpu.VMEM((8, 8, 16, 768), f32),
            pltpu.VMEM((4, 128, 768), f32),
            pltpu.VMEM((16, 16, 768), bf16),
            pltpu.VMEM((16, 16, 128), jnp.int32),
            pltpu.VMEM((16, 1024), f32),
            pltpu.VMEM((256, 1024), f32),
            pltpu.VMEM((256, 1024), bf16),
            pltpu.VMEM((2, 8, 16, HALF), f32),
            pltpu.VMEM((2, 2, 4, 8, 16, HALF), bf16),
            pltpu.VMEM((2, 2, 4, 8, 16, HALF), bf16),
            pltpu.VMEM((2, 8, 16, HALF), bf16),
            pltpu.VMEM((2, 8, 16, HALF), bf16),
            pltpu.VMEM((4, 128, 768), bf16),
            pltpu.VMEM((4, 128, 768), bf16),
            pltpu.VMEM((2, 4, 64, 768), bf16),
            pltpu.VMEM((2, 4, 64, 768), bf16),
            dma((10,)),
            dma((16 * SUBS,)),
            dma((16 * SUBS,)),
            dma((16,)),
            dma((16,)),
            dma((4,)),
            dma((4,)),
            dma((8,)),
            dma((8,)),
        ],
        compiler_params=pltpu.CompilerParams(
            collective_id=0, has_side_effects=True, vmem_limit_bytes=40 * 1024 * 1024
        ),
        cost_estimate=pl.CostEstimate(
            flops=6 * 1024 * 1024 * 768, bytes_accessed=4 * 1024 * 1024, transcendentals=1024 * 1024
        ),
    )(*given)
    small = pltpu.CompilerParams(vmem_limit_bytes=2 * 1024 * 1024)
    return pl.pallas_call(hand_over, out_shape=outs, in_specs=[vmem, vmem], out_specs=(vmem, vmem), compiler_params=small)(*found)


def solution(mesh):
    in_specs = (P("dp", None), P("label", None), P("label"), P("dp", None), P("dp", None))
    out_specs = (P(("dp", "label"), None), P(("label", "dp"), None))
    return jax.shard_map(on_device, mesh=mesh, in_specs=in_specs, out_specs=out_specs, check_vma=False)
```
